32 devices in a mesh: group: 2 (over y), seq: 4 (over z), dp: 2 (over x), head: 2 (over core).
Axes of the slice: x: 2, y: 2, z: 4, core: 2. Of those that a mesh axis runs over, the one named last changes fastest.
Arguments:
- gdn_query: bfloat16 [4, 512, 2048], P(('group', 'dp'), 'seq', 'head'), parts along dimension 0, may hold values from -6 to 6
- gdn_key: bfloat16 [4, 512, 2048], P(('group', 'dp'), 'seq', 'head'), parts along dimension 0, may hold values from -6 to 6
- gdn_value: bfloat16 [4, 512, 2048], P(('group', 'dp'), 'seq', 'head'), parts along dimension 0, may hold values from -6 to 6
- gdn_cot: bfloat16 [4, 512, 2048], P(('group', 'dp'), 'seq', 'head'), parts along dimension 0, may hold values from -6 to 6
- gate_log: float32 [4, 16, 512], P(('group', 'dp'), 'head', 'seq'), parts along dimension 0, may hold values from -1 to 0, as said below
- beta: float32 [4, 16, 512], P(('group', 'dp'), 'head', 'seq'), parts along dimension 0, may hold values from 0 to 1
- state_in: float32 [4, 4, 16, 128, 128], P(('group', 'dp'), 'seq', 'head'), parts along dimension 0, may hold values from -3 to 3
- gdn_rot: bfloat16 [16, 128, 128], P('head'), may hold values from -0.5 to 0.5
- att_query: bfloat16 [4, 512, 2048], P(('group', 'dp'), 'seq', 'head'), parts along dimension 0, may hold values from -130 to 130
- att_key: bfloat16 [4, 512, 1024], P(('group', 'dp'), 'seq', 'head'), parts along dimension 0, may hold values from -7 to 7
- att_value: bfloat16 [4, 512, 1024], P(('group', 'dp'), 'seq', 'head'), parts along dimension 0, may hold values from -6 to 6
- att_cot: bfloat16 [4, 512, 2048], P(('group', 'dp'), 'seq', 'head'), parts along dimension 0, may hold values from -6 to 6
- att_rot: bfloat16 [16, 128, 128], P('head'), may hold values from -0.5 to 0.5
Outputs:
- gdn_query_grad: bfloat16 [4, 512, 2048], P(('group', 'dp'), 'seq', 'head'), parts along dimension 0
- gdn_key_grad: bfloat16 [4, 512, 2048], P(('group', 'dp'), 'seq', 'head'), parts along dimension 0
- gdn_value_grad: bfloat16 [4, 512, 2048], P(('group', 'dp'), 'seq', 'head'), parts along dimension 0
- gate_grad: float32 [4, 16, 512], P(('group', 'dp'), 'head', 'seq'), parts along dimension 0
- beta_grad: float32 [4, 16, 512], P(('group', 'dp'), 'head', 'seq'), parts along dimension 0
- gdn_rot_grad: float32 [32, 128, 128], P(('group', 'head'), 'dp'), parts along dimension 0
- att_query_grad: bfloat16 [4, 512, 2048], P(('group', 'dp'), 'seq', 'head'), parts along dimension 0
- att_key_grad: bfloat16 [4, 512, 1024], P(('group', 'dp'), 'seq', 'head'), parts along dimension 0
- att_value_grad: bfloat16 [4, 512, 1024], P(('group', 'dp'), 'seq', 'head'), parts along dimension 0
- att_rot_grad: float32 [32, 128, 128], P(('group', 'head'), 'dp'), parts along dimension 0
The draws below stay inside these ranges and needn't reach their ends.
There are 2 independent parts, one for each index of `group`. The reference program is written for one: setup_inputs(seed, part) draws one part's arguments, and reference() takes and returns one part's arrays. A program takes and returns all parts, laid end to end along the dimension named above; an argument that names none is the same for every part. Nothing has to cross between parts.
Inputs may be any that keep to these rules, and one draw needn't show every extreme that they name: gate_log is never positive.
All inputs are finite; a program needn't handle non-finite values.
Results may differ from the reference program's by a relative error of at most 0.008.
Values may be sent and summed in bfloat16 or wider, within the bound.
A program may use at most 192 MiB of HBM per device.

```python
import jax
import jax.numpy as jnp
from jax import lax

HEADS = 16
KV_HEADS = 8
HEAD_DIM = 128
WINDOW = 256
TOK_DEV = 128
SEQS = 2
STRING_LENGTH = 512
SHARDS = 4
N_SEQ = 4


def gate_pair(base_key):
    folded = jax.random.fold_in(base_key, 71)
    streams = jax.random.split(folded, 8)
    slow_share = 0.5
    slow_heads = jax.random.uniform(streams[0], (SEQS, HEADS, 1)) < slow_share
    total_tokens = STRING_LENGTH * 1.0
    slow_rate = jax.random.uniform(streams[1], (SEQS, HEADS, 1), minval=0.3, maxval=1.5) / total_tokens
    fast_rate = jax.random.uniform(streams[2], (SEQS, HEADS, 1), minval=1.0 / 50.0, maxval=1.0 / 30.0)
    jitter = jax.random.uniform(streams[3], (SEQS, HEADS, STRING_LENGTH), minval=0.5, maxval=1.5)
    forgetting_factors = jnp.where(slow_heads, slow_rate, fast_rate) * jitter
    place_indices = jax.random.randint(streams[4], (SEQS, 1, 4), 0, STRING_LENGTH)
    spike_exists = jnp.any(jnp.arange(STRING_LENGTH)[None, None, None, :] == place_indices[..., None], axis=2)
    stack_count_total = jax.random.uniform(streams[5], (SEQS, HEADS, STRING_LENGTH), minval=0.22, maxval=0.69)
    forget_factor_items = -forgetting_factors - jnp.where(spike_exists, stack_count_total, 0.0)
    slow_beta = jax.random.uniform(streams[6], (SEQS, HEADS, STRING_LENGTH), minval=0.3, maxval=1.0) * (HEAD_DIM / total_tokens)
    fast_beta = jax.random.uniform(streams[7], (SEQS, HEADS, STRING_LENGTH), minval=0.3, maxval=0.9)
    beta_values = jnp.where(slow_heads, slow_beta, fast_beta)
    return (forget_factor_items.astype(jnp.float32), beta_values.astype(jnp.float32))


def draw_gate_log(key, part):
    return gate_pair(key)[0]


def draw_beta(key, part):
    return gate_pair(key)[1]


def query_key_pair(base_key):
    folded = jax.random.fold_in(base_key, 83)
    streams = jax.random.split(folded, 2)
    keys_drawn = jax.random.truncated_normal(streams[0], -6.0, 6.0, (SEQS, STRING_LENGTH, KV_HEADS * HEAD_DIM))
    queries = jax.random.truncated_normal(streams[1], -6.0, 6.0, (SEQS, STRING_LENGTH, HEADS * HEAD_DIM))
    return (queries, keys_drawn)


def draw_att_query(key, part):
    return query_key_pair(key)[0].astype(jnp.bfloat16)


def draw_att_key(key, part):
    return query_key_pair(key)[1].astype(jnp.bfloat16)


def shard_levels(key, shape, cuts, smallest, high):
    def one(axis_at, blocks):
        draws = jax.random.uniform(jax.random.fold_in(jax.random.fold_in(key, 6), axis_at), (blocks,), jnp.float32, smallest / len(cuts), high / len(cuts))
        return jnp.repeat(jnp.exp(draws), shape[axis_at] // blocks).reshape((-1,) + (1,) * (len(shape) - axis_at - 1))

    loudness = one(*cuts[0])
    for cut in cuts[1:]:
        loudness = loudness * one(*cut)
    return loudness


def centred(stream_key, extent, scale, most, cuts=(), kind=jnp.bfloat16):
    gain = shard_levels(stream_key, extent, cuts, -0.22, 0.18) if cuts else 1.0
    entries = jax.random.normal(stream_key, extent, jnp.float32) * scale * gain
    return jnp.minimum(jnp.maximum(entries, -most), most).astype(kind)


def setup_inputs(seed: int = 0, part: int = 0) -> dict:
    key_list = jax.random.split(jax.random.key(seed), 14)
    part_keys = jax.random.split(jax.random.fold_in(key_list[13], part), 14)
    return {
        "gdn_query": centred(part_keys[0], (SEQS, STRING_LENGTH, HEADS * HEAD_DIM), 1.0, 6.0, ((0, 2), (1, 4), (2, 2))),
        "gdn_key": centred(part_keys[1], (SEQS, STRING_LENGTH, HEADS * HEAD_DIM), 1.0, 6.0, ((0, 2), (1, 4), (2, 2))),
        "gdn_value": centred(part_keys[2], (SEQS, STRING_LENGTH, HEADS * HEAD_DIM), 1.0, 6.0, ((0, 2), (1, 4), (2, 2))),
        "gdn_cot": centred(part_keys[3], (SEQS, STRING_LENGTH, HEADS * HEAD_DIM), 1.0, 6.0, ((0, 2), (1, 4), (2, 2))),
        "gate_log": draw_gate_log(jax.random.fold_in(jax.random.fold_in(key_list[13], part), 71), part),
        "beta": draw_beta(jax.random.fold_in(jax.random.fold_in(key_list[13], part), 71), part),
        "state_in": centred(part_keys[6], (SEQS, SHARDS, HEADS, HEAD_DIM, HEAD_DIM), 0.5, 3.0, ((0, 2), (1, 4), (2, 2)), jnp.float32),
        "gdn_rot": centred(key_list[7], (HEADS, HEAD_DIM, HEAD_DIM), HEAD_DIM ** -0.5, 0.5, ((0, 2),)),
        "att_query": draw_att_query(jax.random.fold_in(jax.random.fold_in(key_list[13], part), 71), part),
        "att_key": draw_att_key(jax.random.fold_in(jax.random.fold_in(key_list[13], part), 71), part),
        "att_value": centred(part_keys[10], (SEQS, STRING_LENGTH, KV_HEADS * HEAD_DIM), 1.0, 6.0, ((0, 2), (1, 4), (2, 2))),
        "att_cot": centred(part_keys[11], (SEQS, STRING_LENGTH, HEADS * HEAD_DIM), 1.0, 6.0, ((0, 2), (1, 4), (2, 2))),
        "att_rot": centred(key_list[12], (HEADS, HEAD_DIM, HEAD_DIM), HEAD_DIM ** -0.5, 0.5, ((0, 2),)),
    }


NORM_EPSILON = 1e-06
HIGHEST_PRECISION = lax.Precision.HIGHEST
MASK_FLOOR = -1e+30

def unit_rows(values):
    return values / jnp.sqrt(lax.optimization_barrier(jnp.sum(values * values, axis=-1, keepdims=True)) + NORM_EPSILON)

def to_bfloat(values):
    return lax.optimization_barrier(values.astype(jnp.bfloat16)).astype(jnp.float32)

def shard_delta(start_state, query_in, key_in, value_in, gate_in, beta_in):
    query_unit = unit_rows(query_in)
    key_unit = unit_rows(key_in)

    def advance(state_now, pieces):
        query_row, key_row, value_row, gate_row, beta_row = pieces
        held_state = jnp.exp(gate_row)[..., None, None] * state_now
        predicted = jnp.einsum('bhvk,bhk->bhv', held_state, key_row, precision=HIGHEST_PRECISION)
        update = beta_row[..., None] * (value_row - predicted)
        fresh_state = held_state + update[..., :, None] * key_row[..., None, :]
        output = jnp.einsum('bhvk,bhk->bhv', fresh_state, query_row, precision=HIGHEST_PRECISION)
        return (fresh_state, output)
    pieces = tuple((jnp.moveaxis(member, 2, 0) for member in (query_unit, key_unit, value_in, gate_in, beta_in)))
    final_state, outputs = lax.scan(advance, start_state, pieces)
    return (jnp.moveaxis(outputs, 0, 2), final_state)

def gdn_backward(gdn_query, gdn_key, gdn_value, gdn_cot, gate_log, beta, state_in, gdn_rot):
    seq_rows = gdn_query.shape[0]

    def shard_major(array):
        shaped = array.astype(jnp.float32).reshape(seq_rows, N_SEQ, TOK_DEV, HEADS, HEAD_DIM)
        return jnp.transpose(shaped, (1, 0, 3, 2, 4))

    def gate_major(array):
        return jnp.transpose(array.reshape(seq_rows, HEADS, N_SEQ, TOK_DEV), (2, 0, 1, 3))
    cot_major = shard_major(gdn_cot)
    out_grad = to_bfloat(jnp.einsum('cshta,hab->cshtb', cot_major, gdn_rot.astype(jnp.float32)))
    pieces = (jnp.moveaxis(state_in, 1, 0), shard_major(gdn_query), shard_major(gdn_key), shard_major(gdn_value), gate_major(gate_log), gate_major(beta), out_grad)

    def back_step(later_grad, members):
        start_state, query_in, key_in, value_in, gate_in, beta_in, grad_in = members
        primal, pullback = jax.vjp(shard_delta, start_state, query_in, key_in, value_in, gate_in, beta_in)
        grads = pullback((grad_in, later_grad))
        return (grads[0], (primal[0], grads[1], grads[2], grads[3], grads[4], grads[5]))
    zero_state = jnp.zeros((seq_rows, HEADS, HEAD_DIM, HEAD_DIM), jnp.float32)
    first_grad, stacked = lax.scan(back_step, zero_state, pieces, reverse=True)
    outputs, grad_query, grad_key, grad_value, grad_gate, grad_beta = stacked

    def token_major(array):
        return jnp.transpose(array, (1, 0, 3, 2, 4)).reshape(seq_rows, STRING_LENGTH, HEADS * HEAD_DIM).astype(jnp.bfloat16)

    def gate_back(array):
        return jnp.transpose(array, (1, 2, 0, 3)).reshape(seq_rows, HEADS, STRING_LENGTH)
    rot_grad = jnp.einsum('cshta,cshtb->hab', cot_major, to_bfloat(outputs))
    return (token_major(grad_query), token_major(grad_key), token_major(grad_value), gate_back(grad_gate), gate_back(grad_beta), rot_grad)

def window_softmax_reverse(att_query, att_key, att_value, att_cot, att_rot):
    seq_rows = att_query.shape[0]
    group_size = HEADS // KV_HEADS
    key_span = WINDOW + TOK_DEV
    kv_width = KV_HEADS * HEAD_DIM
    score_scale = HEAD_DIM ** (-0.5)
    pad_spec = ((0, 0), (WINDOW, 0), (0, 0))
    key_pad = jnp.pad(att_key.astype(jnp.float32), pad_spec)
    value_pad = jnp.pad(att_value.astype(jnp.float32), pad_spec)
    rotation = att_rot.astype(jnp.float32).reshape(KV_HEADS, group_size, HEAD_DIM, HEAD_DIM)

    def block(carry, portion_number):
        key_grad, value_grad, rot_grad = carry
        first_row = portion_number * TOK_DEV
        query_block = lax.dynamic_slice_in_dim(att_query, first_row, TOK_DEV, 1).astype(jnp.float32).reshape(seq_rows, TOK_DEV, KV_HEADS, group_size, HEAD_DIM)
        cot_block = lax.dynamic_slice_in_dim(att_cot, first_row, TOK_DEV, 1).astype(jnp.float32).reshape(seq_rows, TOK_DEV, KV_HEADS, group_size, HEAD_DIM)
        key_block = lax.dynamic_slice_in_dim(key_pad, first_row, key_span, 1).reshape(seq_rows, key_span, KV_HEADS, HEAD_DIM)
        value_block = lax.dynamic_slice_in_dim(value_pad, first_row, key_span, 1).reshape(seq_rows, key_span, KV_HEADS, HEAD_DIM)
        out_grad = to_bfloat(jnp.einsum('stkga,kgab->stkgb', cot_block, rotation))
        scores = score_scale * jnp.einsum('stkgd,sukd->skgtu', query_block, key_block)
        query_pos = first_row + jnp.arange(TOK_DEV, dtype=jnp.int32)
        key_pos = first_row - WINDOW + jnp.arange(key_span, dtype=jnp.int32)
        allowed = (key_pos[None, :] <= query_pos[:, None]) & (key_pos[None, :] > query_pos[:, None] - WINDOW) & (key_pos[None, :] >= 0)
        scores = jnp.where(allowed, scores, MASK_FLOOR)
        row_top = lax.optimization_barrier(jnp.max(scores, axis=-1, keepdims=True))
        weights = jnp.exp(scores - row_top)
        softmax_rows = weights / lax.optimization_barrier(jnp.sum(weights, axis=-1, keepdims=True))
        probs_low = to_bfloat(softmax_rows)
        output = jnp.einsum('skgtu,sukd->stkgd', probs_low, value_block)
        prob_grad = jnp.einsum('stkgd,sukd->skgtu', out_grad, value_block)
        row_dot = lax.optimization_barrier(jnp.sum(softmax_rows * prob_grad, axis=-1, keepdims=True))
        dscore_low = to_bfloat(softmax_rows * (prob_grad - row_dot))
        query_grad = (score_scale * jnp.einsum('skgtu,sukd->stkgd', dscore_low, key_block)).astype(jnp.bfloat16)
        key_term = to_bfloat(score_scale * jnp.einsum('skgtu,stkgd->sukd', dscore_low, query_block)).reshape(seq_rows, key_span, kv_width)
        value_term = to_bfloat(jnp.einsum('skgtu,stkgd->sukd', probs_low, out_grad)).reshape(seq_rows, key_span, kv_width)
        key_grad = lax.dynamic_update_slice_in_dim(key_grad, lax.dynamic_slice_in_dim(key_grad, first_row, key_span, 1) + key_term, first_row, 1)
        value_grad = lax.dynamic_update_slice_in_dim(value_grad, lax.dynamic_slice_in_dim(value_grad, first_row, key_span, 1) + value_term, first_row, 1)
        rot_grad = rot_grad + jnp.einsum('stkga,stkgb->kgab', cot_block, to_bfloat(output))
        return ((key_grad, value_grad, rot_grad), query_grad.reshape(seq_rows, TOK_DEV, HEADS * HEAD_DIM))
    zero_pad = jnp.zeros((seq_rows, WINDOW + STRING_LENGTH, kv_width), jnp.float32)
    zero_rot = jnp.zeros((KV_HEADS, group_size, HEAD_DIM, HEAD_DIM), jnp.float32)
    carry, query_grads = lax.scan(block, (zero_pad, zero_pad, zero_rot), jnp.arange(N_SEQ, dtype=jnp.int32))
    key_grad, value_grad, rot_grad = carry
    query_grad = jnp.transpose(query_grads, (1, 0, 2, 3)).reshape(seq_rows, STRING_LENGTH, HEADS * HEAD_DIM)
    return (query_grad, key_grad[:, WINDOW:].astype(jnp.bfloat16), value_grad[:, WINDOW:].astype(jnp.bfloat16), rot_grad.reshape(HEADS, HEAD_DIM, HEAD_DIM))

def reference(gdn_query, gdn_key, gdn_value, gdn_cot, gate_log, beta, state_in, gdn_rot, att_query, att_key, att_value, att_cot, att_rot):
    gdn_q_grad, gdn_k_grad, gdn_v_grad, gate_grad, beta_grad, gdn_rot_grad = gdn_backward(gdn_query, gdn_key, gdn_value, gdn_cot, gate_log, beta, state_in, gdn_rot)
    att_q_grad, att_k_grad, att_v_grad, att_rot_grad = window_softmax_reverse(att_query, att_key, att_value, att_cot, att_rot)
    return (gdn_q_grad, gdn_k_grad, gdn_v_grad, gate_grad, beta_grad, gdn_rot_grad, att_q_grad, att_k_grad, att_v_grad, att_rot_grad)
```

```python
import functools

import jax
import jax.numpy as jnp
from jax import lax
from jax.experimental import pallas as pl
from jax.experimental.pallas import tpu as pltpu
from jax.sharding import PartitionSpec as P

WINDOW = 256
NORM_EPSILON = 1e-06
MASK_FLOOR = -1e30
F32 = jnp.float32
BF16 = jnp.bfloat16
NN = ((1,), (0,))
NT = ((1,), (1,))
TN = ((0,), (0,))
INVERSE_PASSES = 3
PASSES = 3


def dot(a, b, dims):
    return lax.dot_general(a, b, (dims, ((), ())), preferred_element_type=F32)


def parts_of(a, passes):
    if a.dtype == BF16:
        return (a,)
    high = a.astype(BF16)
    if passes == 1:
        return (high,)
    return (high, (a - high.astype(F32)).astype(BF16))


def mm(a, b, dims, passes=None):
    passes = PASSES if passes is None else passes
    left, right = parts_of(a, passes), parts_of(b, passes)
    total = dot(left[0], right[0], dims)
    if len(left) > 1:
        total = total + dot(left[1], right[0], dims)
    if len(right) > 1:
        total = total + dot(left[0], right[1], dims)
    return total


def lockstep(steps):
    steps = list(steps)
    while steps:
        alive = []
        for step in steps:
            try:
                next(step)
                alive.append(step)
            except StopIteration:
                pass
        steps = alive


def token_facts(q, k, gate, beta):
    rows = q.shape[0]
    t = lax.broadcasted_iota(jnp.int32, (rows, rows), 0)
    s = lax.broadcasted_iota(jnp.int32, (rows, rows), 1)
    eye, within, strict = t == s, t >= s, t > s
    pick = lambda mask, x, axis: jnp.sum(jnp.where(mask, x, 0.0), axis=axis, keepdims=True)
    gate_col = pick(eye, gate, 1)
    beta_col = pick(eye, beta, 1)
    sum_col = pick(within, gate, 1)
    sum_row = pick(t <= s, gate_col, 0)
    last = sum_col[rows - 1 : rows]
    ratios = jnp.where(within, jnp.exp(jnp.where(within, sum_col - sum_row, 0.0)), 0.0)
    qf, kf = q.astype(F32), k.astype(F32)
    rq = 1.0 / jnp.sqrt(jnp.sum(qf * qf, axis=1, keepdims=True) + NORM_EPSILON)
    rk = 1.0 / jnp.sqrt(jnp.sum(kf * kf, axis=1, keepdims=True) + NORM_EPSILON)
    rk_row = pick(eye, rk, 0)
    kk = dot(k, k, NT) * (rk * rk_row)
    qk = dot(q, k, NT) * (rq * rk_row)
    return dict(
        t=t, s=s, eye=eye, within=within, strict=strict, pick=pick, beta=beta_col,
        decay=jnp.exp(sum_col), last=last, tail=jnp.exp(last - sum_col), ratios=ratios,
        rq=rq, rk=rk, qn=qf * rq, kn=kf * rk, kk=kk, qk=qk,
    )


def ahead_kernel(per, q_ref, k_ref, v_ref, cot_ref, gate_ref, beta_ref, state_ref, rot_ref,
                 local_ref, move_ref, w_ref, y_ref, z_ref, ks_ref, qs_ref, grad_ref, term_ref):
    first = pl.program_id(1) * per

    def head(i):
        lanes = slice(i * 128, (i + 1) * 128)
        q, k, v, cot = (r[0, :, lanes] for r in (q_ref, k_ref, v_ref, cot_ref))
        gate = gate_ref[0, pl.ds(first + i, 1), :]
        beta = beta_ref[0, pl.ds(first + i, 1), :]
        out_grad = dot(cot, rot_ref[i], NN).astype(BF16)
        grad_ref[0, i] = out_grad
        f = token_facts(q, k, gate, beta)
        yield
        state = state_ref[0, 0, i]
        seen_k = mm(k, state, NT) * f["rk"]
        seen_q = mm(q, state, NT) * f["rq"]
        ks_ref[0, i] = seen_k
        qs_ref[0, i] = seen_q
        lower = jnp.where(f["strict"], f["beta"] * f["ratios"] * f["kk"], 0.0)
        t, s = f["t"], f["s"]
        rows = q.shape[0]
        inverse = jnp.where(f["eye"], 1.0, 0.0)
        size = 1
        while size < rows:
            mask = (t // (2 * size) == s // (2 * size)) & (t // size != s // size)
            part = jnp.where(mask, lower, 0.0)
            if size == 1:
                inverse = inverse - part
            else:
                half = mm(part, inverse, NN, INVERSE_PASSES)
                yield
                inverse = inverse - mm(inverse, half, NN, INVERSE_PASSES)
                yield
            size *= 2
        bd = f["beta"] * f["decay"]
        x = mm(inverse, bd * f["kn"], NN)
        w = mm(inverse, f["beta"] * v.astype(F32) - bd * seen_k, NN)
        probs = f["ratios"] * f["qk"]
        tail_k = f["tail"] * f["kn"]
        yield
        w_ref[0, i] = w
        seen = mm(probs, out_grad, TN)
        z = mm(inverse, tail_k, TN)
        z_ref[0, i] = z
        out = f["decay"] * seen_q + mm(probs, w, NN)
        term_ref[i] = dot(cot, out.astype(BF16), TN)
        yield
        y = mm(inverse, seen, TN)
        y_ref[0, i] = y
        keep = jnp.exp(f["last"])
        move_ref[0, i] = jnp.where(f["eye"], keep, 0.0) - mm(tail_k, x, TN)
        yield
        og = f["decay"] * out_grad.astype(F32)
        local_ref[0, i] = mm(og, f["qn"], TN) - mm(bd * y, f["kn"], TN)

    lockstep(head(i) for i in range(per))


def back_kernel(per, q_ref, k_ref, v_ref, gate_ref, beta_ref, state_ref,
                later_ref, w_ref, y_ref, z_ref, ks_ref, qs_ref, grad_ref,
                dq_ref, dk_ref, dv_ref, dgate_ref, dbeta_ref):
    first = pl.program_id(1) * per

    def head(i):
        lanes = slice(i * 128, (i + 1) * 128)
        q, k, v = (r[0, :, lanes] for r in (q_ref, k_ref, v_ref))
        at = pl.ds(first + i, 1)
        f = token_facts(q, k, gate_ref[0, at, :], beta_ref[0, at, :])
        later = later_ref[0, i]
        state = state_ref[0, 0, i]
        w, seen_k, seen_q, out_grad = w_ref[0, i], ks_ref[0, i], qs_ref[0, i], grad_ref[0, i]
        pick, eye, within, strict = f["pick"], f["eye"], f["within"], f["strict"]
        total = lambda x: jnp.sum(x, axis=1, keepdims=True)
        dr = y_ref[0, i] + mm(z_ref[0, i], later, NT)
        wh = f["tail"] * mm(w, later, NN)
        dp = jnp.where(within, mm(out_grad, w, NT), 0.0)
        yield
        da = jnp.where(strict, -mm(dr, w, NT), 0.0)
        og = f["decay"] * out_grad.astype(F32)
        dks = -(f["beta"] * f["decay"]) * dr
        yield
        dqk = dp * f["ratios"]
        dar = da * f["ratios"]
        dkk = f["beta"] * dar
        dark = dar * f["kk"]
        e = f["beta"] * dark + dqk * f["qk"]
        dkn = mm(dks, state, NN) + mm(dkk, f["kn"], NN) + wh
        dqn = mm(og, state, NN) + mm(dqk, f["kn"], NN)
        yield
        dkn = dkn + mm(dkk, f["kn"], TN) + mm(dqk, f["qn"], TN)
        yield
        vf = v.astype(F32)
        dbeta = total(dark) + total(dr * (vf - f["decay"] * seen_k))
        carried = total(f["kn"] * wh)
        dsum = total(e) + total(og * seen_q + dks * seen_k) - carried
        dsum = dsum - pick(eye, jnp.sum(e, axis=0, keepdims=True), 1)
        end = jnp.sum(carried, axis=0, keepdims=True) + jnp.exp(f["last"]) * jnp.sum(
            total(later * state), axis=0, keepdims=True
        )
        dgate_ref[0, at, :] = pick(within, dsum, 0) + end
        dbeta_ref[0, at, :] = pick(eye, dbeta, 0)
        dv_ref[0, :, lanes] = (f["beta"] * dr).astype(BF16)
        dq_ref[0, :, lanes] = (f["rq"] * (dqn - f["qn"] * total(f["qn"] * dqn))).astype(BF16)
        dk_ref[0, :, lanes] = (f["rk"] * (dkn - f["kn"] * total(f["kn"] * dkn))).astype(BF16)

    lockstep(head(i) for i in range(per))


def window_kernel(reach, group, place_ref, q_ref, cot_ref, rot_ref, *refs):
    keys = jnp.concatenate([r[0] for r in refs[: reach + 1]], axis=0)
    values = jnp.concatenate([r[0] for r in refs[reach + 1 : 2 * reach + 2]], axis=0)
    dq_ref, term_ref = refs[2 * reach + 2 : 2 * reach + 4]
    key_outs = refs[2 * reach + 4 : 3 * reach + 5]
    value_outs = refs[3 * reach + 5 :]
    rows = q_ref.shape[1]
    scale = 128 ** (-0.5)
    t = lax.broadcasted_iota(jnp.int32, (rows, keys.shape[0]), 0)
    u = lax.broadcasted_iota(jnp.int32, (rows, keys.shape[0]), 1) - reach * rows
    allowed = (u <= t) & (u > t - WINDOW) & (u + place_ref[0, 0] * rows >= 0)
    key_sum, value_sum = [], []

    def head(g):
        lanes = slice(g * 128, (g + 1) * 128)
        q, cot = q_ref[0, :, lanes], cot_ref[0, :, lanes]
        out_grad = dot(cot, rot_ref[g], NN).astype(BF16)
        scores = jnp.where(allowed, scale * dot(q, keys, NT), MASK_FLOOR)
        yield
        prob_grad = dot(out_grad, values, NT)
        weights = jnp.exp(scores - jnp.max(scores, axis=1, keepdims=True))
        probs = weights / jnp.sum(weights, axis=1, keepdims=True)
        low = probs.astype(BF16)
        yield
        out = dot(low, values, NN)
        row_dot = jnp.sum(probs * prob_grad, axis=1, keepdims=True)
        dscore = (probs * (prob_grad - row_dot)).astype(BF16)
        yield
        dq_ref[0, :, lanes] = (scale * dot(dscore, keys, NN)).astype(BF16)
        key_sum.append(dot(dscore, q, TN))
        value_sum.append(dot(low, out_grad, TN))
        term_ref[g] = dot(cot, out.astype(BF16), TN)

    lockstep(head(g) for g in range(group))
    key_term = (scale * functools.reduce(jnp.add, key_sum)).astype(BF16)
    value_term = functools.reduce(jnp.add, value_sum).astype(BF16)
    for j in range(reach + 1):
        key_outs[j][0] = key_term[j * rows : (j + 1) * rows]
        value_outs[j][0] = value_term[j * rows : (j + 1) * rows]


def per_head(shape, per):
    return pl.BlockSpec((1, per) + shape, lambda b, h: (b, h, 0, 0))


def shifted(x, by):
    size = lax.axis_size("seq")
    return lax.ppermute(x, "seq", [(i, i + by) for i in range(size) if 0 <= i + by < size])


def body(gdn_query, gdn_key, gdn_value, gdn_cot, gate_log, beta, state_in, gdn_rot,
         att_query, att_key, att_value, att_cot, att_rot):
    rows_s, tokens, width = gdn_query.shape
    heads = gdn_rot.shape[0]
    n_seq = lax.axis_size("seq")
    kv_width = att_key.shape[2]
    kv_count = kv_width // 128
    group = heads // kv_count
    reach = -(-WINDOW // tokens)
    per = 4
    params = pltpu.CompilerParams(vmem_limit_bytes=48 * 2**20)
    flops = 2 * heads * 128**3

    keys = [shifted(att_key, d) for d in range(reach, 0, -1)] + [att_key]
    values = [shifted(att_value, d) for d in range(reach, 0, -1)] + [att_value]

    tok = pl.BlockSpec((1, tokens, per * 128), lambda b, h: (b, 0, h))
    gate_spec = pl.BlockSpec((1, heads, tokens), lambda b, h: (b, 0, 0))
    state_spec = pl.BlockSpec((1, 1, per, 128, 128), lambda b, h: (b, 0, h, 0, 0))
    rot_spec = pl.BlockSpec((per, 128, 128), lambda b, h: (h, 0, 0))
    square, token_wide = per_head((128, 128), per), per_head((tokens, 128), per)
    like = lambda *shape, dtype=F32: jax.ShapeDtypeStruct(shape, dtype)
    wide = like(rows_s, heads, tokens, 128)
    mat = like(rows_s, heads, 128, 128)

    local, move, w, y, z, ks, qs, grad, gdn_term = pl.pallas_call(
        functools.partial(ahead_kernel, per),
        name="ahead",
        grid=(rows_s, heads // per),
        in_specs=[tok] * 4 + [gate_spec] * 2 + [state_spec, rot_spec],
        out_specs=[square] * 2 + [token_wide] * 6 + [rot_spec],
        out_shape=[mat, mat, wide, wide, wide, wide, wide,
                   like(rows_s, heads, tokens, 128, dtype=BF16), like(heads, 128, 128)],
        compiler_params=params,
        cost_estimate=pl.CostEstimate(flops=80 * flops, bytes_accessed=6 * 2**20, transcendentals=0),
    )(gdn_query, gdn_key, gdn_value, gdn_cot, gate_log, beta, state_in, gdn_rot)

    travel = BF16 if n_seq <= 8 else F32
    later = shifted(local.astype(travel), -1)
    for _ in range(n_seq - 2):
        carried = local + jnp.einsum(
            "bhvk,bhkl->bhvl", later.astype(F32), move, precision=lax.Precision.HIGH
        )
        later = shifted(carried.astype(travel), -1)
    later = later.astype(F32)

    q_spec = pl.BlockSpec((1, tokens, group * 128), lambda b, h: (b, 0, h))
    kv_spec = pl.BlockSpec((1, tokens, 128), lambda b, h: (b, 0, h))
    group_spec = pl.BlockSpec((group, 128, 128), lambda b, h: (h, 0, 0))
    kv_out = like(rows_s, tokens, kv_width, dtype=BF16)
    place = jnp.full((1, 1), lax.axis_index("seq"), jnp.int32)
    outs = pl.pallas_call(
        functools.partial(window_kernel, reach, group),
        name="window",
        grid=(rows_s, kv_count),
        in_specs=[pl.BlockSpec(memory_space=pltpu.SMEM), q_spec, q_spec, group_spec]
        + [kv_spec] * (2 * reach + 2),
        out_specs=[q_spec, group_spec] + [kv_spec] * (2 * reach + 2),
        out_shape=[like(rows_s, tokens, width, dtype=BF16), like(heads, 128, 128)]
        + [kv_out] * (2 * reach + 2),
        compiler_params=params,
        cost_estimate=pl.CostEstimate(flops=60 * flops, bytes_accessed=4 * 2**20, transcendentals=0),
    )(place, att_query, att_cot, att_rot, *keys, *values)
    att_dq, att_term = outs[:2]
    key_terms, value_terms = outs[2 : reach + 3], outs[reach + 3 :]
    dk, dv = key_terms[reach].astype(F32), value_terms[reach].astype(F32)
    for d in range(1, reach + 1):
        dk = dk + shifted(key_terms[reach - d], -d).astype(F32)
        dv = dv + shifted(value_terms[reach - d], -d).astype(F32)

    both = jnp.concatenate([gdn_term, att_term], axis=0)
    share = lax.psum(lax.psum_scatter(both, "dp", scatter_dimension=1, tiled=True), "seq")

    dq_spec = like(rows_s, tokens, width, dtype=BF16)
    gates = like(rows_s, heads, tokens)
    gdn_dq, gdn_dk, gdn_dv, dgate, dbeta = pl.pallas_call(
        functools.partial(back_kernel, per),
        name="back",
        grid=(rows_s, heads // per),
        in_specs=[tok] * 3 + [gate_spec] * 2 + [state_spec, square] + [token_wide] * 6,
        out_specs=[tok] * 3 + [gate_spec] * 2,
        out_shape=[dq_spec] * 3 + [gates] * 2,
        compiler_params=params,
        cost_estimate=pl.CostEstimate(flops=60 * flops, bytes_accessed=6 * 2**20, transcendentals=0),
    )(gdn_query, gdn_key, gdn_value, gate_log, beta, state_in, later, w, y, z, ks, qs, grad)

    return (gdn_dq, gdn_dk, gdn_dv, dgate, dbeta, share[:heads],
            att_dq, dk.astype(BF16), dv.astype(BF16), share[heads:])


def solution(mesh):
    tokens = P(("group", "dp"), "seq", "head")
    gates = P(("group", "dp"), "head", "seq")
    rot = P("head", None, None)
    rot_grad = P(("group", "head"), "dp", None)
    return jax.shard_map(
        body,
        mesh=mesh,
        in_specs=(tokens,) * 4
        + (gates,) * 2
        + (P(("group", "dp"), "seq", "head", None, None), rot)
        + (tokens,) * 4
        + (rot,),
        out_specs=(tokens,) * 3 + (gates,) * 2 + (rot_grad,) + (tokens,) * 3 + (rot_grad,),
        check_vma=False,
    )
```

```python
import functools

import jax
import jax.numpy as jnp
from jax import lax
from jax.experimental import pallas as pl
from jax.experimental.pallas import tpu as pltpu
from jax.sharding import PartitionSpec as P

WINDOW = 256
NORM_EPSILON = 1e-06
MASK_FLOOR = -1e30
F32 = jnp.float32
BF16 = jnp.bfloat16
NN = ((1,), (0,))
NT = ((1,), (1,))
TN = ((0,), (0,))
INVERSE_PASSES = 3
PASSES = 3


def dot(a, b, dims):
    return lax.dot_general(a, b, (dims, ((), ())), preferred_element_type=F32)


def parts_of(a, passes):
    if a.dtype == BF16:
        return (a,)
    high = a.astype(BF16)
    if passes == 1:
        return (high,)
    return (high, (a - high.astype(F32)).astype(BF16))


def mm(a, b, dims, passes=None):
    passes = PASSES if passes is None else passes
    left, right = parts_of(a, passes), parts_of(b, passes)
    total = dot(left[0], right[0], dims)
    if len(left) > 1:
        total = total + dot(left[1], right[0], dims)
    if len(right) > 1:
        total = total + dot(left[0], right[1], dims)
    return total


def lockstep(steps):
    steps = list(steps)
    while steps:
        alive = []
        for step in steps:
            try:
                next(step)
                alive.append(step)
            except StopIteration:
                pass
        steps = alive


def token_facts(q, k, gate, beta):
    rows = q.shape[0]
    t = lax.broadcasted_iota(jnp.int32, (rows, rows), 0)
    s = lax.broadcasted_iota(jnp.int32, (rows, rows), 1)
    eye, within, strict = t == s, t >= s, t > s
    pick = lambda mask, x, axis: jnp.sum(jnp.where(mask, x, 0.0), axis=axis, keepdims=True)
    gate_col = pick(eye, gate, 1)
    beta_col = pick(eye, beta, 1)
    sum_col = pick(within, gate, 1)
    sum_row = pick(t <= s, gate_col, 0)
    last = sum_col[rows - 1 : rows]
    ratios = jnp.where(within, jnp.exp(jnp.where(within, sum_col - sum_row, 0.0)), 0.0)
    qf, kf = q.astype(F32), k.astype(F32)
    rq = 1.0 / jnp.sqrt(jnp.sum(qf * qf, axis=1, keepdims=True) + NORM_EPSILON)
    rk = 1.0 / jnp.sqrt(jnp.sum(kf * kf, axis=1, keepdims=True) + NORM_EPSILON)
    rk_row = pick(eye, rk, 0)
    kk = dot(k, k, NT) * (rk * rk_row)
    qk = dot(q, k, NT) * (rq * rk_row)
    return dict(
        t=t, s=s, eye=eye, within=within, strict=strict, pick=pick, beta=beta_col,
        decay=jnp.exp(sum_col), last=last, tail=jnp.exp(last - sum_col), ratios=ratios,
        rq=rq, rk=rk, qn=qf * rq, kn=kf * rk, kk=kk, qk=qk,
    )


def ahead_kernel(per, q_ref, k_ref, v_ref, cot_ref, gate_ref, beta_ref, state_ref, rot_ref,
                 local_ref, move_ref, w_ref, y_ref, z_ref, ks_ref, qs_ref, grad_ref, term_ref):
    first = pl.program_id(1) * per

    def head(i):
        lanes = slice(i * 128, (i + 1) * 128)
        q, k, v, cot = (r[0, :, lanes] for r in (q_ref, k_ref, v_ref, cot_ref))
        gate = gate_ref[0, pl.ds(first + i, 1), :]
        beta = beta_ref[0, pl.ds(first + i, 1), :]
        out_grad = dot(cot, rot_ref[i], NN).astype(BF16)
        grad_ref[0, i] = out_grad
        f = token_facts(q, k, gate, beta)
        yield
        state = state_ref[0, 0, i]
        seen_k = mm(k, state, NT) * f["rk"]
        seen_q = mm(q, state, NT) * f["rq"]
        ks_ref[0, i] = seen_k
        qs_ref[0, i] = seen_q
        lower = jnp.where(f["strict"], f["beta"] * f["ratios"] * f["kk"], 0.0)
        t, s = f["t"], f["s"]
        rows = q.shape[0]
        inverse = jnp.where(f["eye"], 1.0, 0.0)
        size = 1
        while size < rows:
            mask = (t // (2 * size) == s // (2 * size)) & (t // size != s // size)
            part = jnp.where(mask, lower, 0.0)
            if size == 1:
                inverse = inverse - part
            else:
                half = mm(part, inverse, NN, INVERSE_PASSES)
                yield
                inverse = inverse - mm(inverse, half, NN, INVERSE_PASSES)
                yield
            size *= 2
        bd = f["beta"] * f["decay"]
        x = mm(inverse, bd * f["kn"], NN)
        w = mm(inverse, f["beta"] * v.astype(F32) - bd * seen_k, NN)
        probs = f["ratios"] * f["qk"]
        tail_k = f["tail"] * f["kn"]
        yield
        w_ref[0, i] = w
        seen = mm(probs, out_grad, TN)
        z = mm(inverse, tail_k, TN)
        z_ref[0, i] = z
        out = f["decay"] * seen_q + mm(probs, w, NN)
        term_ref[i] = dot(cot, out.astype(BF16), TN)
        yield
        y = mm(inverse, seen, TN)
        y_ref[0, i] = y
        keep = jnp.exp(f["last"])
        move_ref[0, i] = jnp.where(f["eye"], keep, 0.0) - mm(tail_k, x, TN)
        yield
        og = f["decay"] * out_grad.astype(F32)
        local_ref[0, i] = mm(og, f["qn"], TN) - mm(bd * y, f["kn"], TN)

    lockstep(head(i) for i in range(per))


def back_kernel(per, q_ref, k_ref, v_ref, gate_ref, beta_ref, state_ref,
                later_ref, w_ref, y_ref, z_ref, ks_ref, qs_ref, grad_ref,
                dq_ref, dk_ref, dv_ref, dgate_ref, dbeta_ref):
    first = pl.program_id(1) * per

    def head(i):
        lanes = slice(i * 128, (i + 1) * 128)
        q, k, v = (r[0, :, lanes] for r in (q_ref, k_ref, v_ref))
        at = pl.ds(first + i, 1)
        f = token_facts(q, k, gate_ref[0, at, :], beta_ref[0, at, :])
        later = later_ref[0, i]
        state = state_ref[0, 0, i]
        w, seen_k, seen_q, out_grad = w_ref[0, i], ks_ref[0, i], qs_ref[0, i], grad_ref[0, i]
        pick, eye, within, strict = f["pick"], f["eye"], f["within"], f["strict"]
        total = lambda x: jnp.sum(x, axis=1, keepdims=True)
        dr = y_ref[0, i] + mm(z_ref[0, i], later, NT)
        wh = f["tail"] * mm(w, later, NN)
        dp = jnp.where(within, mm(out_grad, w, NT), 0.0)
        yield
        da = jnp.where(strict, -mm(dr, w, NT), 0.0)
        og = f["decay"] * out_grad.astype(F32)
        dks = -(f["beta"] * f["decay"]) * dr
        yield
        dqk = dp * f["ratios"]
        dar = da * f["ratios"]
        dkk = f["beta"] * dar
        dark = dar * f["kk"]
        e = f["beta"] * dark + dqk * f["qk"]
        dkn = mm(dks, state, NN) + mm(dkk, f["kn"], NN) + wh
        dqn = mm(og, state, NN) + mm(dqk, f["kn"], NN)
        yield
        dkn = dkn + mm(dkk, f["kn"], TN) + mm(dqk, f["qn"], TN)
        yield
        vf = v.astype(F32)
        dbeta = total(dark) + total(dr * (vf - f["decay"] * seen_k))
        carried = total(f["kn"] * wh)
        dsum = total(e) + total(og * seen_q + dks * seen_k) - carried
        dsum = dsum - pick(eye, jnp.sum(e, axis=0, keepdims=True), 1)
        end = jnp.sum(carried, axis=0, keepdims=True) + jnp.exp(f["last"]) * jnp.sum(
            total(later * state), axis=0, keepdims=True
        )
        dgate_ref[0, at, :] = pick(within, dsum, 0) + end
        dbeta_ref[0, at, :] = pick(eye, dbeta, 0)
        dv_ref[0, :, lanes] = (f["beta"] * dr).astype(BF16)
        dq_ref[0, :, lanes] = (f["rq"] * (dqn - f["qn"] * total(f["qn"] * dqn))).astype(BF16)
        dk_ref[0, :, lanes] = (f["rk"] * (dkn - f["kn"] * total(f["kn"] * dkn))).astype(BF16)

    lockstep(head(i) for i in range(per))


def middle_kernel(n, d_size, reach, group, travel, q_ref, cot_ref, rot_ref, k_ref, v_ref,
                  local_ref, move_ref, gterm_ref,
                  dq_ref, dk_ref, dv_ref, later_ref, share_ref,
                  halo, carried, later, term_out, term_in, own_term, rot_all, rot_out, rot_in,
                  part, part_out, part_in, final,
                  halo_s, halo_r, chain_s, chain_r, term_s, term_r, rot_s, rot_r, ps, pr, fs, fr):
    me, x = lax.axis_index("seq"), lax.axis_index("dp")
    rows = q_ref.shape[1]
    heads = local_ref.shape[1]
    kv_count = k_ref.shape[2] // 128
    slab = 128 // d_size
    piece = 2 * heads * slab // n
    scale = 128 ** (-0.5)

    def remote(src, dst, send, recv, axis, peer):
        return pltpu.make_async_remote_copy(
            src_ref=src, dst_ref=dst, send_sem=send, recv_sem=recv,
            device_id={axis: peer}, device_id_type=pl.DeviceIdType.MESH,
        )

    barrier = pltpu.get_barrier_semaphore()
    for k in range(1, n):
        pl.semaphore_signal(barrier, inc=1, device_id={"seq": lax.rem(me + k, n)},
                            device_id_type=pl.DeviceIdType.MESH)
    for k in range(1, d_size):
        pl.semaphore_signal(barrier, inc=1, device_id={"dp": lax.rem(x + k, d_size)},
                            device_id_type=pl.DeviceIdType.MESH)
    pl.semaphore_wait(barrier, n - 1 + d_size - 1)

    def halo_copy(d, j):
        return remote((k_ref, v_ref)[j].at[0], halo.at[d - 1, j], halo_s.at[d - 1, j],
                      halo_r.at[d - 1, j], "seq", lax.rem(me + d, n))

    def chain_copy(h):
        return remote(carried.at[h], later.at[h], chain_s.at[h], chain_r.at[h], "seq",
                      lax.rem(me + n - 1, n))

    def term_copy(d, j):
        return remote(term_out.at[d - 1, j], term_in.at[d - 1, j], term_s.at[d - 1, j],
                      term_r.at[d - 1, j], "seq", lax.rem(me + n - d, n))

    def rot_copy(j, k):
        peer = lax.rem(x + k, d_size)
        at = pl.ds(pl.multiple_of(peer * slab, slab), slab)
        return remote(rot_out.at[j, :, at, :], rot_in.at[k - 1, j],
                      rot_s.at[k - 1, j], rot_r.at[k - 1, j], "dp", peer)

    def piece_at(peer):
        return pl.ds(pl.multiple_of(peer * piece, piece), piece)

    def part_copy(k):
        peer = lax.rem(me + k, n)
        return remote(part_out.at[piece_at(peer)], part_in.at[k - 1], ps.at[k - 1], pr.at[k - 1],
                      "seq", peer)

    def final_copy(k):
        peer = lax.rem(me + k, n)
        return remote(final.at[0], final.at[k], fs.at[k - 1], fr.at[k - 1], "seq", peer)

    for d in range(1, reach + 1):
        @pl.when(me + d < n)
        def _():
            for j in range(2):
                halo_copy(d, j).start()

    @pl.when(me == n - 1)
    def _():
        later[...] = jnp.zeros_like(later)
        for h in range(heads):
            carried[h] = local_ref[0, h].astype(travel)
            chain_copy(h).start()

    rot_out[0] = gterm_ref[...].astype(BF16)
    for k in range(1, d_size):
        rot_copy(0, k).start()

    for d in range(1, reach + 1):
        @pl.when(me < d)
        def _():
            halo[d - 1] = jnp.zeros(halo.shape[1:], halo.dtype)

        @pl.when(me >= d)
        def _():
            for j in range(2):
                halo_copy(d, j).wait_recv()

    span = (reach + 1) * rows
    t = lax.broadcasted_iota(jnp.int32, (rows, span), 0)
    u = lax.broadcasted_iota(jnp.int32, (rows, span), 1) - reach * rows
    allowed = (u <= t) & (u > t - WINDOW) & (u + me * rows >= 0)

    def key_head(c):
        kv_lanes = slice(c * 128, (c + 1) * 128)
        keys = jnp.concatenate(
            [halo[d - 1, 0, :, kv_lanes] for d in range(reach, 0, -1)] + [k_ref[0, :, kv_lanes]], axis=0)
        values = jnp.concatenate(
            [halo[d - 1, 1, :, kv_lanes] for d in range(reach, 0, -1)] + [v_ref[0, :, kv_lanes]], axis=0)
        key_sum, value_sum = 0.0, 0.0
        for g in range(group):
            head = c * group + g
            lanes = slice(head * 128, (head + 1) * 128)
            q, cot = q_ref[0, :, lanes], cot_ref[0, :, lanes]
            out_grad = dot(cot, rot_ref[head], NN).astype(BF16)
            scores = jnp.where(allowed, scale * dot(q, keys, NT), MASK_FLOOR)
            yield
            prob_grad = dot(out_grad, values, NT)
            weights = jnp.exp(scores - jnp.max(scores, axis=1, keepdims=True))
            probs = weights / jnp.sum(weights, axis=1, keepdims=True)
            low = probs.astype(BF16)
            yield
            out = dot(low, values, NN)
            row_dot = jnp.sum(probs * prob_grad, axis=1, keepdims=True)
            dscore = (probs * (prob_grad - row_dot)).astype(BF16)
            yield
            dq_ref[0, :, lanes] = (scale * dot(dscore, keys, NN)).astype(BF16)
            key_sum += dot(dscore, q, TN)
            value_sum += dot(low, out_grad, TN)
            term = dot(cot, out.astype(BF16), TN)
            rot_all[head] = term
            rot_out[1, head] = term.astype(BF16)
            yield
        for j, whole in enumerate(((scale * key_sum).astype(BF16), value_sum.astype(BF16))):
            for d in range(1, reach + 1):
                term_out[d - 1, j, :, kv_lanes] = whole[(reach - d) * rows : (reach - d + 1) * rows]
            own_term[j, :, kv_lanes] = whole[reach * rows :]

    lockstep(key_head(c) for c in range(kv_count))
    for k in range(1, d_size):
        rot_copy(1, k).start()

    for h in range(heads):
        @pl.when(me < n - 1)
        def _():
            chain_copy(h).wait_recv()

            @pl.when(me > 0)
            def _():
                carried[h] = (local_ref[0, h] + mm(later[h].astype(F32), move_ref[0, h], NN)).astype(travel)
                chain_copy(h).start()

    for d in range(1, reach + 1):
        @pl.when(me >= d)
        def _():
            for j in range(2):
                term_copy(d, j).start()

    own = pl.ds(pl.multiple_of(x * slab, slab), slab)
    for j, terms in enumerate((gterm_ref, rot_all)):
        for k in range(1, d_size):
            rot_copy(j, k).wait_recv()
        total = terms[:, own, :]
        for k in range(1, d_size):
            total = total + rot_in[k - 1, j].astype(F32)
        flat = total.reshape(heads * slab, 128)
        part[j * heads * slab : (j + 1) * heads * slab] = flat
        part_out[j * heads * slab : (j + 1) * heads * slab] = flat.astype(BF16)
    for k in range(1, n):
        part_copy(k).start()
    later_ref[0] = later[...].astype(F32)
    for k in range(1, n):
        part_copy(k).wait_recv()
    mine = part[piece_at(me)]
    for k in range(1, n):
        mine = mine + part_in[k - 1].astype(F32)
    final[0] = mine.astype(BF16)
    share_ref[piece_at(me)] = mine
    for k in range(1, n):
        final_copy(k).start()

    for j, out in enumerate((dk_ref, dv_ref)):
        for d in range(1, reach + 1):
            @pl.when(me + d < n)
            def _():
                term_copy(d, j).wait_recv()

            @pl.when(me + d >= n)
            def _():
                term_in[d - 1, j] = jnp.zeros(term_in.shape[2:], BF16)
        total = own_term[j].astype(F32)
        for d in range(1, reach + 1):
            total = total + term_in[d - 1, j].astype(F32)
        out[0] = total.astype(BF16)

    for k in range(1, n):
        final_copy(k).wait_recv()
        share_ref[piece_at(lax.rem(me + n - k, n))] = final[k].astype(F32)

    for k in range(1, n):
        part_copy(k).wait_send()
        final_copy(k).wait_send()
    for j in range(2):
        for k in range(1, d_size):
            rot_copy(j, k).wait_send()
        for d in range(1, reach + 1):
            @pl.when(me + d < n)
            def _():
                halo_copy(d, j).wait_send()

            @pl.when(me >= d)
            def _():
                term_copy(d, j).wait_send()

    @pl.when(me > 0)
    def _():
        for h in range(heads):
            chain_copy(h).wait_send()


def per_head(shape, per):
    return pl.BlockSpec((1, per) + shape, lambda b, h: (b, h, 0, 0))


def body(gdn_query, gdn_key, gdn_value, gdn_cot, gate_log, beta, state_in, gdn_rot,
         att_query, att_key, att_value, att_cot, att_rot):
    rows_s, tokens, width = gdn_query.shape
    heads = gdn_rot.shape[0]
    n_seq = lax.axis_size("seq")
    kv_width = att_key.shape[2]
    kv_count = kv_width // 128
    group = heads // kv_count
    reach = -(-WINDOW // tokens)
    per = 4
    params = pltpu.CompilerParams(vmem_limit_bytes=48 * 2**20)
    flops = 2 * heads * 128**3

    tok = pl.BlockSpec((1, tokens, per * 128), lambda b, h: (b, 0, h))
    gate_spec = pl.BlockSpec((1, heads, tokens), lambda b, h: (b, 0, 0))
    state_spec = pl.BlockSpec((1, 1, per, 128, 128), lambda b, h: (b, 0, h, 0, 0))
    rot_spec = pl.BlockSpec((per, 128, 128), lambda b, h: (h, 0, 0))
    square, token_wide = per_head((128, 128), per), per_head((tokens, 128), per)
    like = lambda *shape, dtype=F32: jax.ShapeDtypeStruct(shape, dtype)
    wide = like(rows_s, heads, tokens, 128)
    mat = like(rows_s, heads, 128, 128)

    local, move, w, y, z, ks, qs, grad, gdn_term = pl.pallas_call(
        functools.partial(ahead_kernel, per),
        name="ahead",
        grid=(rows_s, heads // per),
        in_specs=[tok] * 4 + [gate_spec] * 2 + [state_spec, rot_spec],
        out_specs=[square] * 2 + [token_wide] * 6 + [rot_spec],
        out_shape=[mat, mat, wide, wide, wide, wide, wide,
                   like(rows_s, heads, tokens, 128, dtype=BF16), like(heads, 128, 128)],
        compiler_params=params,
        cost_estimate=pl.CostEstimate(flops=80 * flops, bytes_accessed=6 * 2**20, transcendentals=0),
    )(gdn_query, gdn_key, gdn_value, gdn_cot, gate_log, beta, state_in, gdn_rot)

    travel = BF16 if n_seq <= 8 else F32
    d_size = lax.axis_size("dp")
    slab = 128 // d_size
    piece = 2 * heads * slab // n_seq
    vmem = pl.BlockSpec(memory_space=pltpu.VMEM)
    sem = pltpu.SemaphoreType.DMA
    kv_out = like(rows_s, tokens, kv_width, dtype=BF16)
    att_dq, dk, dv, later, share = pl.pallas_call(
        functools.partial(middle_kernel, n_seq, d_size, reach, group, travel),
        name="middle",
        in_specs=[vmem] * 8,
        out_specs=[vmem] * 5,
        out_shape=[like(rows_s, tokens, width, dtype=BF16), kv_out, kv_out, mat,
                   like(2 * heads * slab, 128)],
        scratch_shapes=[
            pltpu.VMEM((reach, 2, tokens, kv_width), BF16),
            pltpu.VMEM((heads, 128, 128), travel),
            pltpu.VMEM((heads, 128, 128), travel),
            pltpu.VMEM((reach, 2, tokens, kv_width), BF16),
            pltpu.VMEM((reach, 2, tokens, kv_width), BF16),
            pltpu.VMEM((2, tokens, kv_width), BF16),
            pltpu.VMEM((heads, 128, 128), F32),
            pltpu.VMEM((2, heads, 128, 128), BF16),
            pltpu.VMEM((d_size - 1, 2, heads, slab, 128), BF16),
            pltpu.VMEM((2 * heads * slab, 128), F32),
            pltpu.VMEM((2 * heads * slab, 128), BF16),
            pltpu.VMEM((n_seq - 1, piece, 128), BF16),
            pltpu.VMEM((n_seq, piece, 128), BF16),
            sem((reach, 2)), sem((reach, 2)), sem((heads,)), sem((heads,)),
            sem((reach, 2)), sem((reach, 2)), sem((d_size - 1, 2)), sem((d_size - 1, 2)),
            sem((n_seq - 1,)), sem((n_seq - 1,)), sem((n_seq - 1,)), sem((n_seq - 1,)),
        ],
        compiler_params=pltpu.CompilerParams(
            collective_id=0, has_side_effects=True, vmem_limit_bytes=48 * 2**20
        ),
    )(att_query, att_cot, att_rot, att_key, att_value, local, move, gdn_term)
    share = share.reshape(2 * heads, slab, 128)

    dq_spec = like(rows_s, tokens, width, dtype=BF16)
    gates = like(rows_s, heads, tokens)
    gdn_dq, gdn_dk, gdn_dv, dgate, dbeta = pl.pallas_call(
        functools.partial(back_kernel, per),
        name="back",
        grid=(rows_s, heads // per),
        in_specs=[tok] * 3 + [gate_spec] * 2 + [state_spec, square] + [token_wide] * 6,
        out_specs=[tok] * 3 + [gate_spec] * 2,
        out_shape=[dq_spec] * 3 + [gates] * 2,
        compiler_params=params,
        cost_estimate=pl.CostEstimate(flops=60 * flops, bytes_accessed=6 * 2**20, transcendentals=0),
    )(gdn_query, gdn_key, gdn_value, gate_log, beta, state_in, later, w, y, z, ks, qs, grad)

    return (gdn_dq, gdn_dk, gdn_dv, dgate, dbeta, share[:heads],
            att_dq, dk, dv, share[heads:])


def solution(mesh):
    tokens = P(("group", "dp"), "seq", "head")
    gates = P(("group", "dp"), "head", "seq")
    rot = P("head", None, None)
    rot_grad = P(("group", "head"), "dp", None)
    return jax.shard_map(
        body,
        mesh=mesh,
        in_specs=(tokens,) * 4
        + (gates,) * 2
        + (P(("group", "dp"), "seq", "head", None, None), rot)
        + (tokens,) * 4
        + (rot,),
        out_specs=(tokens,) * 3 + (gates,) * 2 + (rot_grad,) + (tokens,) * 3 + (rot_grad,),
        check_vma=False,
    )
```

```python
import functools

import jax
import jax.numpy as jnp
from jax import lax
from jax.experimental import pallas as pl
from jax.experimental.pallas import tpu as pltpu
from jax.sharding import PartitionSpec as P

WINDOW = 256
NORM_EPSILON = 1e-06
MASK_FLOOR = -1e30
F32 = jnp.float32
BF16 = jnp.bfloat16
NN = ((1,), (0,))
NT = ((1,), (1,))
TN = ((0,), (0,))
INVERSE_PASSES = 3
PASSES = 3


def dot(a, b, dims):
    return lax.dot_general(a, b, (dims, ((), ())), preferred_element_type=F32)


def parts_of(a, passes):
    if a.dtype == BF16:
        return (a,)
    high = a.astype(BF16)
    if passes == 1:
        return (high,)
    return (high, (a - high.astype(F32)).astype(BF16))


def mm(a, b, dims, passes=None):
    passes = PASSES if passes is None else passes
    left, right = parts_of(a, passes), parts_of(b, passes)
    total = dot(left[0], right[0], dims)
    if len(left) > 1:
        total = total + dot(left[1], right[0], dims)
    if len(right) > 1:
        total = total + dot(left[0], right[1], dims)
    return total


def lockstep(steps):
    steps = list(steps)
    while steps:
        alive = []
        for step in steps:
            try:
                next(step)
                alive.append(step)
            except StopIteration:
                pass
        steps = alive


def token_facts(q, k, gate, beta):
    rows = q.shape[0]
    t = lax.broadcasted_iota(jnp.int32, (rows, rows), 0)
    s = lax.broadcasted_iota(jnp.int32, (rows, rows), 1)
    eye, within, strict = t == s, t >= s, t > s
    pick = lambda mask, x, axis: jnp.sum(jnp.where(mask, x, 0.0), axis=axis, keepdims=True)
    gate_col = pick(eye, gate, 1)
    beta_col = pick(eye, beta, 1)
    sum_col = pick(within, gate, 1)
    sum_row = pick(t <= s, gate_col, 0)
    last = sum_col[rows - 1 : rows]
    ratios = jnp.where(within, jnp.exp(jnp.where(within, sum_col - sum_row, 0.0)), 0.0)
    qf, kf = q.astype(F32), k.astype(F32)
    rq = 1.0 / jnp.sqrt(jnp.sum(qf * qf, axis=1, keepdims=True) + NORM_EPSILON)
    rk = 1.0 / jnp.sqrt(jnp.sum(kf * kf, axis=1, keepdims=True) + NORM_EPSILON)
    rk_row = pick(eye, rk, 0)
    kk = dot(k, k, NT) * (rk * rk_row)
    qk = dot(q, k, NT) * (rq * rk_row)
    return dict(
        t=t, s=s, eye=eye, within=within, strict=strict, pick=pick, beta=beta_col,
        decay=jnp.exp(sum_col), last=last, tail=jnp.exp(last - sum_col), ratios=ratios,
        rq=rq, rk=rk, qn=qf * rq, kn=kf * rk, kk=kk, qk=qk,
    )


def ahead_heads(chosen, q_ref, k_ref, v_ref, cot_ref, gate_ref, beta_ref, state_ref, rot_ref,
                 local_ref, move_ref, w_ref, y_ref, z_ref, ks_ref, qs_ref, grad_ref, term_ref):
    def head(i):
        lanes = slice(i * 128, (i + 1) * 128)
        q, k, v, cot = (r[0, :, lanes] for r in (q_ref, k_ref, v_ref, cot_ref))
        gate = gate_ref[0, i : i + 1, :]
        beta = beta_ref[0, i : i + 1, :]
        out_grad = dot(cot, rot_ref[i], NN).astype(BF16)
        grad_ref[0, i] = out_grad
        f = token_facts(q, k, gate, beta)
        yield
        state = state_ref[0, 0, i]
        seen_k = mm(k, state, NT) * f["rk"]
        seen_q = mm(q, state, NT) * f["rq"]
        ks_ref[0, i] = seen_k
        qs_ref[0, i] = seen_q
        lower = jnp.where(f["strict"], f["beta"] * f["ratios"] * f["kk"], 0.0)
        t, s = f["t"], f["s"]
        rows = q.shape[0]
        inverse = jnp.where(f["eye"], 1.0, 0.0)
        size = 1
        while size < rows:
            mask = (t // (2 * size) == s // (2 * size)) & (t // size != s // size)
            part = jnp.where(mask, lower, 0.0)
            if size == 1:
                inverse = inverse - part
            else:
                half = mm(part, inverse, NN, INVERSE_PASSES)
                yield
                inverse = inverse - mm(inverse, half, NN, INVERSE_PASSES)
                yield
            size *= 2
        bd = f["beta"] * f["decay"]
        x = mm(inverse, bd * f["kn"], NN)
        w = mm(inverse, f["beta"] * v.astype(F32) - bd * seen_k, NN)
        probs = f["ratios"] * f["qk"]
        tail_k = f["tail"] * f["kn"]
        yield
        w_ref[0, i] = w
        seen = mm(probs, out_grad, TN)
        z = mm(inverse, tail_k, TN)
        z_ref[0, i] = z
        out = f["decay"] * seen_q + mm(probs, w, NN)
        term_ref[i] = dot(cot, out.astype(BF16), TN)
        yield
        y = mm(inverse, seen, TN)
        y_ref[0, i] = y
        keep = jnp.exp(f["last"])
        move_ref[0, i] = jnp.where(f["eye"], keep, 0.0) - mm(tail_k, x, TN)
        yield
        og = f["decay"] * out_grad.astype(F32)
        local_ref[0, i] = mm(og, f["qn"], TN) - mm(bd * y, f["kn"], TN)

    lockstep(head(i) for i in chosen)


def back_kernel(per, q_ref, k_ref, v_ref, gate_ref, beta_ref, state_ref,
                later_ref, w_ref, y_ref, z_ref, ks_ref, qs_ref, grad_ref,
                dq_ref, dk_ref, dv_ref, dgate_ref, dbeta_ref):
    first = pl.program_id(1) * per

    def head(i):
        lanes = slice(i * 128, (i + 1) * 128)
        q, k, v = (r[0, :, lanes] for r in (q_ref, k_ref, v_ref))
        at = pl.ds(first + i, 1)
        f = token_facts(q, k, gate_ref[0, at, :], beta_ref[0, at, :])
        later = later_ref[0, i]
        state = state_ref[0, 0, i]
        w, seen_k, seen_q, out_grad = w_ref[0, i], ks_ref[0, i], qs_ref[0, i], grad_ref[0, i]
        pick, eye, within, strict = f["pick"], f["eye"], f["within"], f["strict"]
        total = lambda x: jnp.sum(x, axis=1, keepdims=True)
        dr = y_ref[0, i] + mm(z_ref[0, i], later, NT)
        wh = f["tail"] * mm(w, later, NN)
        dp = jnp.where(within, mm(out_grad, w, NT), 0.0)
        yield
        da = jnp.where(strict, -mm(dr, w, NT), 0.0)
        og = f["decay"] * out_grad.astype(F32)
        dks = -(f["beta"] * f["decay"]) * dr
        yield
        dqk = dp * f["ratios"]
        dar = da * f["ratios"]
        dkk = f["beta"] * dar
        dark = dar * f["kk"]
        e = f["beta"] * dark + dqk * f["qk"]
        dkn = mm(dks, state, NN) + mm(dkk, f["kn"], NN) + wh
        dqn = mm(og, state, NN) + mm(dqk, f["kn"], NN)
        yield
        dkn = dkn + mm(dkk, f["kn"], TN) + mm(dqk, f["qn"], TN)
        yield
        vf = v.astype(F32)
        dbeta = total(dark) + total(dr * (vf - f["decay"] * seen_k))
        carried = total(f["kn"] * wh)
        dsum = total(e) + total(og * seen_q + dks * seen_k) - carried
        dsum = dsum - pick(eye, jnp.sum(e, axis=0, keepdims=True), 1)
        end = jnp.sum(carried, axis=0, keepdims=True) + jnp.exp(f["last"]) * jnp.sum(
            total(later * state), axis=0, keepdims=True
        )
        dgate_ref[0, at, :] = pick(within, dsum, 0) + end
        dbeta_ref[0, at, :] = pick(eye, dbeta, 0)
        dv_ref[0, :, lanes] = (f["beta"] * dr).astype(BF16)
        dq_ref[0, :, lanes] = (f["rq"] * (dqn - f["qn"] * total(f["qn"] * dqn))).astype(BF16)
        dk_ref[0, :, lanes] = (f["rk"] * (dkn - f["kn"] * total(f["kn"] * dkn))).astype(BF16)

    lockstep(head(i) for i in range(per))


def middle_kernel(n, d_size, reach, group, per, travel, q_ref, cot_ref, rot_ref, k_ref, v_ref,
                  gq_ref, gk_ref, gv_ref, gcot_ref, gate_ref, beta_ref, state_ref, grot_ref,
                  dq_ref, dk_ref, dv_ref, later_ref, share_ref, w_ref, y_ref, z_ref, ks_ref, qs_ref, grad_ref,
                  local_ref, move_ref, gterm_ref,
                  halo, carried, later, term_out, term_in, own_term, rot_all, rot_out, rot_in,
                  part, part_out, part_in, final,
                  halo_s, halo_r, chain_s, chain_r, term_s, term_r, rot_s, rot_r, ps, pr, fs, fr):
    me, x = lax.axis_index("seq"), lax.axis_index("dp")
    rows = q_ref.shape[1]
    heads = state_ref.shape[2]
    kv_count = k_ref.shape[2] // 128
    slab = 128 // d_size
    piece = 2 * heads * slab // n
    scale = 128 ** (-0.5)

    def remote(src, dst, send, recv, axis, peer):
        return pltpu.make_async_remote_copy(
            src_ref=src, dst_ref=dst, send_sem=send, recv_sem=recv,
            device_id={axis: peer}, device_id_type=pl.DeviceIdType.MESH,
        )

    barrier = pltpu.get_barrier_semaphore()
    for k in range(1, n):
        pl.semaphore_signal(barrier, inc=1, device_id={"seq": lax.rem(me + k, n)},
                            device_id_type=pl.DeviceIdType.MESH)
    for k in range(1, d_size):
        pl.semaphore_signal(barrier, inc=1, device_id={"dp": lax.rem(x + k, d_size)},
                            device_id_type=pl.DeviceIdType.MESH)
    pl.semaphore_wait(barrier, n - 1 + d_size - 1)

    def halo_copy(d, j):
        return remote((k_ref, v_ref)[j].at[0], halo.at[d - 1, j], halo_s.at[d - 1, j],
                      halo_r.at[d - 1, j], "seq", lax.rem(me + d, n))

    def chain_copy(h):
        return remote(carried.at[h], later.at[h], chain_s.at[h], chain_r.at[h], "seq",
                      lax.rem(me + n - 1, n))

    def term_copy(d, j):
        return remote(term_out.at[d - 1, j], term_in.at[d - 1, j], term_s.at[d - 1, j],
                      term_r.at[d - 1, j], "seq", lax.rem(me + n - d, n))

    def rot_copy(j, k):
        peer = lax.rem(x + k, d_size)
        at = pl.ds(pl.multiple_of(peer * slab, slab), slab)
        return remote(rot_out.at[j, :, at, :], rot_in.at[k - 1, j],
                      rot_s.at[k - 1, j], rot_r.at[k - 1, j], "dp", peer)

    def piece_at(peer):
        return pl.ds(pl.multiple_of(peer * piece, piece), piece)

    def part_copy(k):
        peer = lax.rem(me + k, n)
        return remote(part_out.at[piece_at(peer)], part_in.at[k - 1], ps.at[k - 1], pr.at[k - 1],
                      "seq", peer)

    def final_copy(k):
        peer = lax.rem(me + k, n)
        return remote(final.at[0], final.at[k], fs.at[k - 1], fr.at[k - 1], "seq", peer)

    for d in range(1, reach + 1):
        @pl.when(me + d < n)
        def _():
            for j in range(2):
                halo_copy(d, j).start()

    for first in range(0, heads, per):
        ahead_heads(range(first, first + per), gq_ref, gk_ref, gv_ref, gcot_ref, gate_ref, beta_ref,
                    state_ref, grot_ref, local_ref, move_ref, w_ref, y_ref, z_ref, ks_ref, qs_ref,
                    grad_ref, gterm_ref)

    @pl.when(me == n - 1)
    def _():
        later[...] = jnp.zeros_like(later)
        for h in range(heads):
            carried[h] = local_ref[0, h].astype(travel)
            chain_copy(h).start()

    rot_out[0] = gterm_ref[...].astype(BF16)
    for k in range(1, d_size):
        rot_copy(0, k).start()

    for d in range(1, reach + 1):
        @pl.when(me < d)
        def _():
            halo[d - 1] = jnp.zeros(halo.shape[1:], halo.dtype)

        @pl.when(me >= d)
        def _():
            for j in range(2):
                halo_copy(d, j).wait_recv()

    span = (reach + 1) * rows
    t = lax.broadcasted_iota(jnp.int32, (rows, span), 0)
    u = lax.broadcasted_iota(jnp.int32, (rows, span), 1) - reach * rows
    allowed = (u <= t) & (u > t - WINDOW) & (u + me * rows >= 0)

    def key_head(c):
        kv_lanes = slice(c * 128, (c + 1) * 128)
        keys = jnp.concatenate(
            [halo[d - 1, 0, :, kv_lanes] for d in range(reach, 0, -1)] + [k_ref[0, :, kv_lanes]], axis=0)
        values = jnp.concatenate(
            [halo[d - 1, 1, :, kv_lanes] for d in range(reach, 0, -1)] + [v_ref[0, :, kv_lanes]], axis=0)
        key_sum, value_sum = 0.0, 0.0
        for g in range(group):
            head = c * group + g
            lanes = slice(head * 128, (head + 1) * 128)
            q, cot = q_ref[0, :, lanes], cot_ref[0, :, lanes]
            out_grad = dot(cot, rot_ref[head], NN).astype(BF16)
            scores = jnp.where(allowed, scale * dot(q, keys, NT), MASK_FLOOR)
            yield
            prob_grad = dot(out_grad, values, NT)
            weights = jnp.exp(scores - jnp.max(scores, axis=1, keepdims=True))
            probs = weights / jnp.sum(weights, axis=1, keepdims=True)
            low = probs.astype(BF16)
            yield
            out = dot(low, values, NN)
            row_dot = jnp.sum(probs * prob_grad, axis=1, keepdims=True)
            dscore = (probs * (prob_grad - row_dot)).astype(BF16)
            yield
            dq_ref[0, :, lanes] = (scale * dot(dscore, keys, NN)).astype(BF16)
            key_sum += dot(dscore, q, TN)
            value_sum += dot(low, out_grad, TN)
            term = dot(cot, out.astype(BF16), TN)
            rot_all[head] = term
            rot_out[1, head] = term.astype(BF16)
            yield
        for j, whole in enumerate(((scale * key_sum).astype(BF16), value_sum.astype(BF16))):
            for d in range(1, reach + 1):
                term_out[d - 1, j, :, kv_lanes] = whole[(reach - d) * rows : (reach - d + 1) * rows]
            own_term[j, :, kv_lanes] = whole[reach * rows :]

    lockstep(key_head(c) for c in range(kv_count))
    for k in range(1, d_size):
        rot_copy(1, k).start()

    for h in range(heads):
        @pl.when(me < n - 1)
        def _():
            chain_copy(h).wait_recv()

            @pl.when(me > 0)
            def _():
                carried[h] = (local_ref[0, h] + mm(later[h].astype(F32), move_ref[0, h], NN)).astype(travel)
                chain_copy(h).start()

    for d in range(1, reach + 1):
        @pl.when(me >= d)
        def _():
            for j in range(2):
                term_copy(d, j).start()

    own = pl.ds(pl.multiple_of(x * slab, slab), slab)
    for j, terms in enumerate((gterm_ref, rot_all)):
        for k in range(1, d_size):
            rot_copy(j, k).wait_recv()
        total = terms[:, own, :]
        for k in range(1, d_size):
            total = total + rot_in[k - 1, j].astype(F32)
        flat = total.reshape(heads * slab, 128)
        part[j * heads * slab : (j + 1) * heads * slab] = flat
        part_out[j * heads * slab : (j + 1) * heads * slab] = flat.astype(BF16)
    for k in range(1, n):
        part_copy(k).start()
    later_ref[0] = later[...].astype(F32)
    for k in range(1, n):
        part_copy(k).wait_recv()
    mine = part[piece_at(me)]
    for k in range(1, n):
        mine = mine + part_in[k - 1].astype(F32)
    final[0] = mine.astype(BF16)
    share_ref[piece_at(me)] = mine
    for k in range(1, n):
        final_copy(k).start()

    for j, out in enumerate((dk_ref, dv_ref)):
        for d in range(1, reach + 1):
            @pl.when(me + d < n)
            def _():
                term_copy(d, j).wait_recv()

            @pl.when(me + d >= n)
            def _():
                term_in[d - 1, j] = jnp.zeros(term_in.shape[2:], BF16)
        total = own_term[j].astype(F32)
        for d in range(1, reach + 1):
            total = total + term_in[d - 1, j].astype(F32)
        out[0] = total.astype(BF16)

    for k in range(1, n):
        final_copy(k).wait_recv()
        share_ref[piece_at(lax.rem(me + n - k, n))] = final[k].astype(F32)

    for k in range(1, n):
        part_copy(k).wait_send()
        final_copy(k).wait_send()
    for j in range(2):
        for k in range(1, d_size):
            rot_copy(j, k).wait_send()
        for d in range(1, reach + 1):
            @pl.when(me + d < n)
            def _():
                halo_copy(d, j).wait_send()

            @pl.when(me >= d)
            def _():
                term_copy(d, j).wait_send()

    @pl.when(me > 0)
    def _():
        for h in range(heads):
            chain_copy(h).wait_send()


def per_head(shape, per):
    return pl.BlockSpec((1, per) + shape, lambda b, h: (b, h, 0, 0))


def body(gdn_query, gdn_key, gdn_value, gdn_cot, gate_log, beta, state_in, gdn_rot,
         att_query, att_key, att_value, att_cot, att_rot):
    rows_s, tokens, width = gdn_query.shape
    heads = gdn_rot.shape[0]
    n_seq = lax.axis_size("seq")
    kv_width = att_key.shape[2]
    kv_count = kv_width // 128
    group = heads // kv_count
    reach = -(-WINDOW // tokens)
    per = 4
    params = pltpu.CompilerParams(vmem_limit_bytes=48 * 2**20)
    flops = 2 * heads * 128**3

    tok = pl.BlockSpec((1, tokens, per * 128), lambda b, h: (b, 0, h))
    gate_spec = pl.BlockSpec((1, heads, tokens), lambda b, h: (b, 0, 0))
    state_spec = pl.BlockSpec((1, 1, per, 128, 128), lambda b, h: (b, 0, h, 0, 0))
    rot_spec = pl.BlockSpec((per, 128, 128), lambda b, h: (h, 0, 0))
    square, token_wide = per_head((128, 128), per), per_head((tokens, 128), per)
    like = lambda *shape, dtype=F32: jax.ShapeDtypeStruct(shape, dtype)
    wide = like(rows_s, heads, tokens, 128)
    mat = like(rows_s, heads, 128, 128)

    travel = BF16 if n_seq <= 8 else F32
    d_size = lax.axis_size("dp")
    slab = 128 // d_size
    piece = 2 * heads * slab // n_seq
    vmem = pl.BlockSpec(memory_space=pltpu.VMEM)
    sem = pltpu.SemaphoreType.DMA
    kv_out = like(rows_s, tokens, kv_width, dtype=BF16)
    att_dq, dk, dv, later, share, w, y, z, ks, qs, grad = pl.pallas_call(
        functools.partial(middle_kernel, n_seq, d_size, reach, group, per, travel),
        name="middle",
        in_specs=[vmem] * 13,
        out_specs=[vmem] * 11,
        out_shape=[like(rows_s, tokens, width, dtype=BF16), kv_out, kv_out, mat,
                   like(2 * heads * slab, 128), wide, wide, wide, wide, wide,
                   like(rows_s, heads, tokens, 128, dtype=BF16)],
        scratch_shapes=[
            pltpu.VMEM((1, heads, 128, 128), F32),
            pltpu.VMEM((1, heads, 128, 128), F32),
            pltpu.VMEM((heads, 128, 128), F32),
            pltpu.VMEM((reach, 2, tokens, kv_width), BF16),
            pltpu.VMEM((heads, 128, 128), travel),
            pltpu.VMEM((heads, 128, 128), travel),
            pltpu.VMEM((reach, 2, tokens, kv_width), BF16),
            pltpu.VMEM((reach, 2, tokens, kv_width), BF16),
            pltpu.VMEM((2, tokens, kv_width), BF16),
            pltpu.VMEM((heads, 128, 128), F32),
            pltpu.VMEM((2, heads, 128, 128), BF16),
            pltpu.VMEM((d_size - 1, 2, heads, slab, 128), BF16),
            pltpu.VMEM((2 * heads * slab, 128), F32),
            pltpu.VMEM((2 * heads * slab, 128), BF16),
            pltpu.VMEM((n_seq - 1, piece, 128), BF16),
            pltpu.VMEM((n_seq, piece, 128), BF16),
            sem((reach, 2)), sem((reach, 2)), sem((heads,)), sem((heads,)),
            sem((reach, 2)), sem((reach, 2)), sem((d_size - 1, 2)), sem((d_size - 1, 2)),
            sem((n_seq - 1,)), sem((n_seq - 1,)), sem((n_seq - 1,)), sem((n_seq - 1,)),
        ],
        compiler_params=pltpu.CompilerParams(
            collective_id=0, has_side_effects=True, vmem_limit_bytes=48 * 2**20
        ),
    )(att_query, att_cot, att_rot, att_key, att_value,
      gdn_query, gdn_key, gdn_value, gdn_cot, gate_log, beta, state_in, gdn_rot)
    share = share.reshape(2 * heads, slab, 128)

    dq_spec = like(rows_s, tokens, width, dtype=BF16)
    gates = like(rows_s, heads, tokens)
    gdn_dq, gdn_dk, gdn_dv, dgate, dbeta = pl.pallas_call(
        functools.partial(back_kernel, per),
        name="back",
        grid=(rows_s, heads // per),
        in_specs=[tok] * 3 + [gate_spec] * 2 + [state_spec, square] + [token_wide] * 6,
        out_specs=[tok] * 3 + [gate_spec] * 2,
        out_shape=[dq_spec] * 3 + [gates] * 2,
        compiler_params=params,
        cost_estimate=pl.CostEstimate(flops=60 * flops, bytes_accessed=6 * 2**20, transcendentals=0),
    )(gdn_query, gdn_key, gdn_value, gate_log, beta, state_in, later, w, y, z, ks, qs, grad)

    return (gdn_dq, gdn_dk, gdn_dv, dgate, dbeta, share[:heads],
            att_dq, dk, dv, share[heads:])


def solution(mesh):
    tokens = P(("group", "dp"), "seq", "head")
    gates = P(("group", "dp"), "head", "seq")
    rot = P("head", None, None)
    rot_grad = P(("group", "head"), "dp", None)
    return jax.shard_map(
        body,
        mesh=mesh,
        in_specs=(tokens,) * 4
        + (gates,) * 2
        + (P(("group", "dp"), "seq", "head", None, None), rot)
        + (tokens,) * 4
        + (rot,),
        out_specs=(tokens,) * 3 + (gates,) * 2 + (rot_grad,) + (tokens,) * 3 + (rot_grad,),
        check_vma=False,
    )
```

```python
import functools

import jax
import jax.numpy as jnp
from jax import lax
from jax.experimental import pallas as pl
from jax.experimental.pallas import tpu as pltpu
from jax.sharding import PartitionSpec as P

WINDOW = 256
NORM_EPSILON = 1e-06
MASK_FLOOR = -1e30
F32 = jnp.float32
BF16 = jnp.bfloat16
NN = ((1,), (0,))
NT = ((1,), (1,))
TN = ((0,), (0,))
INVERSE_PASSES = 3
PASSES = 3


def dot(a, b, dims):
    return lax.dot_general(a, b, (dims, ((), ())), preferred_element_type=F32)


def parts_of(a, passes):
    if a.dtype == BF16:
        return (a,)
    high = a.astype(BF16)
    if passes == 1:
        return (high,)
    return (high, (a - high.astype(F32)).astype(BF16))


def mm(a, b, dims, passes=None):
    passes = PASSES if passes is None else passes
    left, right = parts_of(a, passes), parts_of(b, passes)
    total = dot(left[0], right[0], dims)
    if len(left) > 1:
        total = total + dot(left[1], right[0], dims)
    if len(right) > 1:
        total = total + dot(left[0], right[1], dims)
    return total


def lockstep(steps):
    steps = list(steps)
    while steps:
        alive = []
        for step in steps:
            try:
                next(step)
                alive.append(step)
            except StopIteration:
                pass
        steps = alive


def token_facts(q, k, gate, beta):
    rows = q.shape[0]
    t = lax.broadcasted_iota(jnp.int32, (rows, rows), 0)
    s = lax.broadcasted_iota(jnp.int32, (rows, rows), 1)
    eye, within, strict = t == s, t >= s, t > s
    pick = lambda mask, x, axis: jnp.sum(jnp.where(mask, x, 0.0), axis=axis, keepdims=True)
    gate_col = pick(eye, gate, 1)
    beta_col = pick(eye, beta, 1)
    sum_col = pick(within, gate, 1)
    sum_row = pick(t <= s, gate_col, 0)
    last = sum_col[rows - 1 : rows]
    ratios = jnp.where(within, jnp.exp(jnp.where(within, sum_col - sum_row, 0.0)), 0.0)
    qf, kf = q.astype(F32), k.astype(F32)
    rq = 1.0 / jnp.sqrt(jnp.sum(qf * qf, axis=1, keepdims=True) + NORM_EPSILON)
    rk = 1.0 / jnp.sqrt(jnp.sum(kf * kf, axis=1, keepdims=True) + NORM_EPSILON)
    rk_row = pick(eye, rk, 0)
    kk = dot(k, k, NT) * (rk * rk_row)
    qk = dot(q, k, NT) * (rq * rk_row)
    return dict(
        t=t, s=s, eye=eye, within=within, strict=strict, pick=pick, beta=beta_col,
        decay=jnp.exp(sum_col), last=last, tail=jnp.exp(last - sum_col), ratios=ratios,
        rq=rq, rk=rk, qn=qf * rq, kn=kf * rk, kk=kk, qk=qk,
    )


def ahead_heads(chosen, q_ref, k_ref, v_ref, cot_ref, gate_ref, beta_ref, state_ref, rot_ref,
                 local_ref, move_ref, w_ref, y_ref, z_ref, ks_ref, qs_ref, grad_ref, term_ref):
    def head(i):
        lanes = slice(i * 128, (i + 1) * 128)
        q, k, v, cot = (r[0, :, lanes] for r in (q_ref, k_ref, v_ref, cot_ref))
        gate = gate_ref[0, i : i + 1, :]
        beta = beta_ref[0, i : i + 1, :]
        out_grad = dot(cot, rot_ref[i], NN).astype(BF16)
        grad_ref[0, i] = out_grad
        f = token_facts(q, k, gate, beta)
        yield
        state = state_ref[0, 0, i]
        seen_k = mm(k, state, NT) * f["rk"]
        seen_q = mm(q, state, NT) * f["rq"]
        ks_ref[0, i] = seen_k
        qs_ref[0, i] = seen_q
        lower = jnp.where(f["strict"], f["beta"] * f["ratios"] * f["kk"], 0.0)
        t, s = f["t"], f["s"]
        rows = q.shape[0]
        inverse = jnp.where(f["eye"], 1.0, 0.0)
        size = 1
        while size < rows:
            mask = (t // (2 * size) == s // (2 * size)) & (t // size != s // size)
            part = jnp.where(mask, lower, 0.0)
            if size == 1:
                inverse = inverse - part
            else:
                half = mm(part, inverse, NN, INVERSE_PASSES)
                yield
                inverse = inverse - mm(inverse, half, NN, INVERSE_PASSES)
                yield
            size *= 2
        bd = f["beta"] * f["decay"]
        x = mm(inverse, bd * f["kn"], NN)
        w = mm(inverse, f["beta"] * v.astype(F32) - bd * seen_k, NN)
        probs = f["ratios"] * f["qk"]
        tail_k = f["tail"] * f["kn"]
        yield
        w_ref[0, i] = w
        seen = mm(probs, out_grad, TN)
        z = mm(inverse, tail_k, TN)
        z_ref[0, i] = z
        out = f["decay"] * seen_q + mm(probs, w, NN)
        term_ref[i] = dot(cot, out.astype(BF16), TN)
        yield
        y = mm(inverse, seen, TN)
        y_ref[0, i] = y
        keep = jnp.exp(f["last"])
        move_ref[0, i] = jnp.where(f["eye"], keep, 0.0) - mm(tail_k, x, TN)
        yield
        og = f["decay"] * out_grad.astype(F32)
        local_ref[0, i] = mm(og, f["qn"], TN) - mm(bd * y, f["kn"], TN)

    lockstep(head(i) for i in chosen)


def back_kernel(per, q_ref, k_ref, v_ref, gate_ref, beta_ref, state_ref,
                later_ref, w_ref, y_ref, z_ref, ks_ref, qs_ref, grad_ref,
                dq_ref, dk_ref, dv_ref, dgate_ref, dbeta_ref):
    first = pl.program_id(1) * per

    def head(i):
        lanes = slice(i * 128, (i + 1) * 128)
        q, k, v = (r[0, :, lanes] for r in (q_ref, k_ref, v_ref))
        at = pl.ds(first + i, 1)
        f = token_facts(q, k, gate_ref[0, at, :], beta_ref[0, at, :])
        later = later_ref[0, i]
        state = state_ref[0, 0, i]
        w, seen_k, seen_q, out_grad = w_ref[0, i], ks_ref[0, i], qs_ref[0, i], grad_ref[0, i]
        pick, eye, within, strict = f["pick"], f["eye"], f["within"], f["strict"]
        total = lambda x: jnp.sum(x, axis=1, keepdims=True)
        dr = y_ref[0, i] + mm(z_ref[0, i], later, NT)
        wh = f["tail"] * mm(w, later, NN)
        dp = jnp.where(within, mm(out_grad, w, NT), 0.0)
        yield
        da = jnp.where(strict, -mm(dr, w, NT), 0.0)
        og = f["decay"] * out_grad.astype(F32)
        dks = -(f["beta"] * f["decay"]) * dr
        yield
        dqk = dp * f["ratios"]
        dar = da * f["ratios"]
        dkk = f["beta"] * dar
        dark = dar * f["kk"]
        e = f["beta"] * dark + dqk * f["qk"]
        dkn = mm(dks, state, NN) + mm(dkk, f["kn"], NN) + wh
        dqn = mm(og, state, NN) + mm(dqk, f["kn"], NN)
        yield
        dkn = dkn + mm(dkk, f["kn"], TN) + mm(dqk, f["qn"], TN)
        yield
        vf = v.astype(F32)
        dbeta = total(dark) + total(dr * (vf - f["decay"] * seen_k))
        carried = total(f["kn"] * wh)
        dsum = total(e) + total(og * seen_q + dks * seen_k) - carried
        dsum = dsum - pick(eye, jnp.sum(e, axis=0, keepdims=True), 1)
        end = jnp.sum(carried, axis=0, keepdims=True) + jnp.exp(f["last"]) * jnp.sum(
            total(later * state), axis=0, keepdims=True
        )
        dgate_ref[0, at, :] = pick(within, dsum, 0) + end
        dbeta_ref[0, at, :] = pick(eye, dbeta, 0)
        dv_ref[0, :, lanes] = (f["beta"] * dr).astype(BF16)
        dq_ref[0, :, lanes] = (f["rq"] * (dqn - f["qn"] * total(f["qn"] * dqn))).astype(BF16)
        dk_ref[0, :, lanes] = (f["rk"] * (dkn - f["kn"] * total(f["kn"] * dkn))).astype(BF16)

    lockstep(head(i) for i in range(per))


def middle_kernel(n, d_size, reach, group, per, travel, q_ref, cot_ref, rot_ref, k_ref, v_ref,
                  gq_ref, gk_ref, gv_ref, gcot_ref, gate_ref, beta_ref, state_ref, grot_ref,
                  dq_ref, dk_ref, dv_ref, later_ref, share_ref, w_ref, y_ref, z_ref, ks_ref, qs_ref, grad_ref,
                  local_ref, move_ref, gterm_ref,
                  halo, carried, later, term_out, term_in, own_term, rot_all, rot_out, rot_in,
                  part, part_out, part_in, final,
                  halo_s, halo_r, chain_s, chain_r, term_s, term_r, rot_s, rot_r, ps, pr, fs, fr):
    me, x = lax.axis_index("seq"), lax.axis_index("dp")
    rows = q_ref.shape[1]
    heads = state_ref.shape[2]
    kv_count = k_ref.shape[2] // 128
    slab = 128 // d_size
    piece = 2 * heads * slab // n
    scale = 128 ** (-0.5)

    def remote(src, dst, send, recv, axis, peer):
        return pltpu.make_async_remote_copy(
            src_ref=src, dst_ref=dst, send_sem=send, recv_sem=recv,
            device_id={axis: peer}, device_id_type=pl.DeviceIdType.MESH,
        )

    barrier = pltpu.get_barrier_semaphore()
    for k in range(1, n):
        pl.semaphore_signal(barrier, inc=1, device_id={"seq": lax.rem(me + k, n)},
                            device_id_type=pl.DeviceIdType.MESH)
    for k in range(1, d_size):
        pl.semaphore_signal(barrier, inc=1, device_id={"dp": lax.rem(x + k, d_size)},
                            device_id_type=pl.DeviceIdType.MESH)
    pl.semaphore_wait(barrier, n - 1 + d_size - 1)

    def halo_copy(d, j):
        return remote((k_ref, v_ref)[j].at[0], halo.at[d - 1, j], halo_s.at[d - 1, j],
                      halo_r.at[d - 1, j], "seq", lax.rem(me + d, n))

    def chain_copy(h):
        return remote(carried.at[h], later.at[h], chain_s.at[h], chain_r.at[h], "seq",
                      lax.rem(me + n - 1, n))

    def term_copy(d, j):
        return remote(term_out.at[d - 1, j], term_in.at[d - 1, j], term_s.at[d - 1, j],
                      term_r.at[d - 1, j], "seq", lax.rem(me + n - d, n))

    def rot_copy(j, k):
        peer = lax.rem(x + k, d_size)
        at = pl.ds(pl.multiple_of(peer * slab, slab), slab)
        return remote(rot_out.at[j, :, at, :], rot_in.at[k - 1, j],
                      rot_s.at[k - 1, j], rot_r.at[k - 1, j], "dp", peer)

    def piece_at(peer):
        return pl.ds(pl.multiple_of(peer * piece, piece), piece)

    def part_copy(k):
        peer = lax.rem(me + k, n)
        return remote(part_out.at[piece_at(peer)], part_in.at[k - 1], ps.at[k - 1], pr.at[k - 1],
                      "seq", peer)

    def final_copy(k):
        peer = lax.rem(me + k, n)
        return remote(final.at[0], final.at[k], fs.at[k - 1], fr.at[k - 1], "seq", peer)

    for d in range(1, reach + 1):
        @pl.when(me + d < n)
        def _():
            for j in range(2):
                halo_copy(d, j).start()

    for first in range(0, heads, per):
        ahead_heads(range(first, first + per), gq_ref, gk_ref, gv_ref, gcot_ref, gate_ref, beta_ref,
                    state_ref, grot_ref, local_ref, move_ref, w_ref, y_ref, z_ref, ks_ref, qs_ref,
                    grad_ref, gterm_ref)

    @pl.when(me == n - 1)
    def _():
        later[...] = jnp.zeros_like(later)
        for h in range(heads):
            carried[h] = local_ref[0, h].astype(travel)
            chain_copy(h).start()

    rot_out[0] = gterm_ref[...].astype(BF16)
    for k in range(1, d_size):
        rot_copy(0, k).start()

    for d in range(1, reach + 1):
        @pl.when(me < d)
        def _():
            halo[d - 1] = jnp.zeros(halo.shape[1:], halo.dtype)

        @pl.when(me >= d)
        def _():
            for j in range(2):
                halo_copy(d, j).wait_recv()

    span = (reach + 1) * rows
    t = lax.broadcasted_iota(jnp.int32, (rows, span), 0)
    u = lax.broadcasted_iota(jnp.int32, (rows, span), 1) - reach * rows
    allowed = (u <= t) & (u > t - WINDOW) & (u + me * rows >= 0)

    def key_head(c):
        kv_lanes = slice(c * 128, (c + 1) * 128)
        keys = jnp.concatenate(
            [halo[d - 1, 0, :, kv_lanes] for d in range(reach, 0, -1)] + [k_ref[0, :, kv_lanes]], axis=0)
        values = jnp.concatenate(
            [halo[d - 1, 1, :, kv_lanes] for d in range(reach, 0, -1)] + [v_ref[0, :, kv_lanes]], axis=0)
        key_sum, value_sum = 0.0, 0.0
        for g in range(group):
            head = c * group + g
            lanes = slice(head * 128, (head + 1) * 128)
            q, cot = q_ref[0, :, lanes], cot_ref[0, :, lanes]
            out_grad = dot(cot, rot_ref[head], NN).astype(BF16)
            scores = jnp.where(allowed, scale * dot(q, keys, NT), MASK_FLOOR)
            yield
            prob_grad = dot(out_grad, values, NT)
            weights = jnp.exp(scores - jnp.max(scores, axis=1, keepdims=True))
            probs = weights / jnp.sum(weights, axis=1, keepdims=True)
            low = probs.astype(BF16)
            yield
            out = dot(low, values, NN)
            row_dot = jnp.sum(probs * prob_grad, axis=1, keepdims=True)
            dscore = (probs * (prob_grad - row_dot)).astype(BF16)
            yield
            dq_ref[0, :, lanes] = (scale * dot(dscore, keys, NN)).astype(BF16)
            key_sum += dot(dscore, q, TN)
            value_sum += dot(low, out_grad, TN)
            term = dot(cot, out.astype(BF16), TN)
            rot_all[head] = term
            rot_out[1, head] = term.astype(BF16)
            yield
        for j, whole in enumerate(((scale * key_sum).astype(BF16), value_sum.astype(BF16))):
            for d in range(1, reach + 1):
                term_out[d - 1, j, :, kv_lanes] = whole[(reach - d) * rows : (reach - d + 1) * rows]
            own_term[j, :, kv_lanes] = whole[reach * rows :]

    lockstep(key_head(c) for c in range(kv_count))
    for k in range(1, d_size):
        rot_copy(1, k).start()

    for d in range(1, reach + 1):
        @pl.when(me >= d)
        def _():
            for j in range(2):
                term_copy(d, j).start()

    for h in range(heads):
        @pl.when(me < n - 1)
        def _():
            chain_copy(h).wait_recv()

            @pl.when(me > 0)
            def _():
                carried[h] = (local_ref[0, h] + mm(later[h].astype(F32), move_ref[0, h], NN)).astype(travel)
                chain_copy(h).start()

    own = pl.ds(pl.multiple_of(x * slab, slab), slab)
    for j, terms in enumerate((gterm_ref, rot_all)):
        for k in range(1, d_size):
            rot_copy(j, k).wait_recv()
        total = terms[:, own, :]
        for k in range(1, d_size):
            total = total + rot_in[k - 1, j].astype(F32)
        flat = total.reshape(heads * slab, 128)
        part[j * heads * slab : (j + 1) * heads * slab] = flat
        part_out[j * heads * slab : (j + 1) * heads * slab] = flat.astype(BF16)
    for k in range(1, n):
        part_copy(k).start()
    later_ref[0] = later[...].astype(F32)
    for k in range(1, n):
        part_copy(k).wait_recv()
    mine = part[piece_at(me)]
    for k in range(1, n):
        mine = mine + part_in[k - 1].astype(F32)
    final[0] = mine.astype(BF16)
    share_ref[piece_at(me)] = mine
    for k in range(1, n):
        final_copy(k).start()

    for j, out in enumerate((dk_ref, dv_ref)):
        for d in range(1, reach + 1):
            @pl.when(me + d < n)
            def _():
                term_copy(d, j).wait_recv()

            @pl.when(me + d >= n)
            def _():
                term_in[d - 1, j] = jnp.zeros(term_in.shape[2:], BF16)
        total = own_term[j].astype(F32)
        for d in range(1, reach + 1):
            total = total + term_in[d - 1, j].astype(F32)
        out[0] = total.astype(BF16)

    for k in range(1, n):
        final_copy(k).wait_recv()
        share_ref[piece_at(lax.rem(me + n - k, n))] = final[k].astype(F32)

    for k in range(1, n):
        part_copy(k).wait_send()
        final_copy(k).wait_send()
    for j in range(2):
        for k in range(1, d_size):
            rot_copy(j, k).wait_send()
        for d in range(1, reach + 1):
            @pl.when(me + d < n)
            def _():
                halo_copy(d, j).wait_send()

            @pl.when(me >= d)
            def _():
                term_copy(d, j).wait_send()

    @pl.when(me > 0)
    def _():
        for h in range(heads):
            chain_copy(h).wait_send()


def per_head(shape, per):
    return pl.BlockSpec((1, per) + shape, lambda b, h: (b, h, 0, 0))


def body(gdn_query, gdn_key, gdn_value, gdn_cot, gate_log, beta, state_in, gdn_rot,
         att_query, att_key, att_value, att_cot, att_rot):
    rows_s, tokens, width = gdn_query.shape
    heads = gdn_rot.shape[0]
    n_seq = lax.axis_size("seq")
    kv_width = att_key.shape[2]
    kv_count = kv_width // 128
    group = heads // kv_count
    reach = -(-WINDOW // tokens)
    per = 4
    params = pltpu.CompilerParams(vmem_limit_bytes=48 * 2**20)
    flops = 2 * heads * 128**3

    tok = pl.BlockSpec((1, tokens, per * 128), lambda b, h: (b, 0, h))
    gate_spec = pl.BlockSpec((1, heads, tokens), lambda b, h: (b, 0, 0))
    state_spec = pl.BlockSpec((1, 1, per, 128, 128), lambda b, h: (b, 0, h, 0, 0))
    rot_spec = pl.BlockSpec((per, 128, 128), lambda b, h: (h, 0, 0))
    square, token_wide = per_head((128, 128), per), per_head((tokens, 128), per)
    like = lambda *shape, dtype=F32: jax.ShapeDtypeStruct(shape, dtype)
    wide = like(rows_s, heads, tokens, 128)
    mat = like(rows_s, heads, 128, 128)

    travel = BF16 if n_seq <= 8 else F32
    d_size = lax.axis_size("dp")
    slab = 128 // d_size
    piece = 2 * heads * slab // n_seq
    vmem = pl.BlockSpec(memory_space=pltpu.VMEM)
    sem = pltpu.SemaphoreType.DMA
    kv_out = like(rows_s, tokens, kv_width, dtype=BF16)
    att_dq, dk, dv, later, share, w, y, z, ks, qs, grad = pl.pallas_call(
        functools.partial(middle_kernel, n_seq, d_size, reach, group, per, travel),
        name="middle",
        in_specs=[vmem] * 13,
        out_specs=[vmem] * 11,
        out_shape=[like(rows_s, tokens, width, dtype=BF16), kv_out, kv_out, mat,
                   like(2 * heads * slab, 128), wide, wide, wide, wide, wide,
                   like(rows_s, heads, tokens, 128, dtype=BF16)],
        scratch_shapes=[
            pltpu.VMEM((1, heads, 128, 128), F32),
            pltpu.VMEM((1, heads, 128, 128), F32),
            pltpu.VMEM((heads, 128, 128), F32),
            pltpu.VMEM((reach, 2, tokens, kv_width), BF16),
            pltpu.VMEM((heads, 128, 128), travel),
            pltpu.VMEM((heads, 128, 128), travel),
            pltpu.VMEM((reach, 2, tokens, kv_width), BF16),
            pltpu.VMEM((reach, 2, tokens, kv_width), BF16),
            pltpu.VMEM((2, tokens, kv_width), BF16),
            pltpu.VMEM((heads, 128, 128), F32),
            pltpu.VMEM((2, heads, 128, 128), BF16),
            pltpu.VMEM((d_size - 1, 2, heads, slab, 128), BF16),
            pltpu.VMEM((2 * heads * slab, 128), F32),
            pltpu.VMEM((2 * heads * slab, 128), BF16),
            pltpu.VMEM((n_seq - 1, piece, 128), BF16),
            pltpu.VMEM((n_seq, piece, 128), BF16),
            sem((reach, 2)), sem((reach, 2)), sem((heads,)), sem((heads,)),
            sem((reach, 2)), sem((reach, 2)), sem((d_size - 1, 2)), sem((d_size - 1, 2)),
            sem((n_seq - 1,)), sem((n_seq - 1,)), sem((n_seq - 1,)), sem((n_seq - 1,)),
        ],
        compiler_params=pltpu.CompilerParams(
            collective_id=0, has_side_effects=True, vmem_limit_bytes=48 * 2**20
        ),
    )(att_query, att_cot, att_rot, att_key, att_value,
      gdn_query, gdn_key, gdn_value, gdn_cot, gate_log, beta, state_in, gdn_rot)
    share = share.reshape(2 * heads, slab, 128)

    dq_spec = like(rows_s, tokens, width, dtype=BF16)
    gates = like(rows_s, heads, tokens)
    gdn_dq, gdn_dk, gdn_dv, dgate, dbeta = pl.pallas_call(
        functools.partial(back_kernel, per),
        name="back",
        grid=(rows_s, heads // per),
        in_specs=[tok] * 3 + [gate_spec] * 2 + [state_spec, square] + [token_wide] * 6,
        out_specs=[tok] * 3 + [gate_spec] * 2,
        out_shape=[dq_spec] * 3 + [gates] * 2,
        compiler_params=params,
        cost_estimate=pl.CostEstimate(flops=60 * flops, bytes_accessed=6 * 2**20, transcendentals=0),
    )(gdn_query, gdn_key, gdn_value, gate_log, beta, state_in, later, w, y, z, ks, qs, grad)

    return (gdn_dq, gdn_dk, gdn_dv, dgate, dbeta, share[:heads],
            att_dq, dk, dv, share[heads:])


def solution(mesh):
    tokens = P(("group", "dp"), "seq", "head")
    gates = P(("group", "dp"), "head", "seq")
    rot = P("head", None, None)
    rot_grad = P(("group", "head"), "dp", None)
    return jax.shard_map(
        body,
        mesh=mesh,
        in_specs=(tokens,) * 4
        + (gates,) * 2
        + (P(("group", "dp"), "seq", "head", None, None), rot)
        + (tokens,) * 4
        + (rot,),
        out_specs=(tokens,) * 3 + (gates,) * 2 + (rot_grad,) + (tokens,) * 3 + (rot_grad,),
        check_vma=False,
    )
```
